32 devices in a mesh: rows: 8 (over z, y), cols: 4 (over x, core).
Axes of the slice: x: 2, y: 2, z: 4, core: 2. Of those that a mesh axis runs over, the one named last changes fastest.
Arguments:
- tracks: float32 [1024, 2, 16384], P(('rows', 'cols')), may hold values from -200 to 200
- pixel_order: int32 [16384], P('rows'), may hold values from 0 to 16383, as said below
- pairing: int32 [2, 4], replicated, may hold values from 0 to 2
Outputs:
- rotated: float32 [16384, 2048], P('rows', 'cols')
The draws below stay inside these ranges and needn't reach their ends.
Inputs may be any that keep to these rules, and one draw needn't show every extreme that they name: `pixel_order`: A permutation of 0 to 16383 that maps each aligned block of 2048 rows onto the same block of pixels.
All inputs are finite; a program needn't handle non-finite values.
Results may differ from the reference program's by a relative error of at most 0.0001.
Values sent between devices are 32-bit elements; how exact they have to be, the bound alone decides.
No kernel may reach another device: no remote copies, remote signals or barrier semaphores. Data moves between devices by JAX's collectives and lax.ppermute only.
A program may use at most 64 MiB of HBM per device.

```python
import math
import jax
import jax.numpy as jnp
from jax import lax

FRAMES = 1024
NBLK = 16
BLK = 128
M_DEV = 2048
PIXELS = 16384
STEPS = 2
NS_STEPS = 6
N_COLS = 4


def draw_tracks(key, part):
    keys = jax.random.split(key, 5)
    rise = 3.0 ** (jnp.arange(PIXELS, dtype=jnp.float32) / PIXELS - 0.5)
    row_scale = rise * jnp.exp(jax.random.uniform(keys[0], (PIXELS,), jnp.float32, math.log(0.5), math.log(2.0)))
    noise = jnp.clip(jax.random.normal(keys[1], (FRAMES, 2, PIXELS), jnp.float32), -5.0, 5.0)
    common = jax.random.uniform(keys[2], (FRAMES, 2, 1), jnp.float32, -0.5, 0.5)
    column_scale = jnp.exp(jax.random.uniform(keys[3], (FRAMES, 2, 1), jnp.float32, math.log(0.3), math.log(3.0)))
    factor = jnp.clip(jax.random.normal(keys[4], (PIXELS,), jnp.float32), -5.0, 5.0)
    return column_scale * row_scale[None, None, :] * (noise + common * factor[None, None, :])


def draw_pixel_order(key, part):
    block_keys = jax.random.split(key, PIXELS // M_DEV)
    shuffled = jax.vmap(lambda single: jax.random.permutation(single, M_DEV))(block_keys)
    offsets = (jnp.arange(PIXELS // M_DEV, dtype=jnp.int32) * M_DEV)[:, None]
    return (shuffled.astype(jnp.int32) + offsets).reshape(PIXELS)


def with_ends(drawn, rng, smallest, largest):
    longest = drawn.shape.index(max(drawn.shape))
    spots = []
    for shift in (0, 1):
        where = [jax.random.randint(jax.random.fold_in(rng, axis), (), 0, length) for axis, length in enumerate(drawn.shape)]
        where[longest] = (where[longest] + shift) % drawn.shape[longest]
        spots.append(tuple(where))
    return drawn.at[spots[0]].set(smallest).at[spots[1]].set(largest)


def setup_inputs(seed: int = 0) -> dict:
    splits = jax.random.split(jax.random.key(seed), 4)
    tracks = draw_tracks(jax.random.fold_in(splits[3], 71), 0)
    pixel_order = draw_pixel_order(jax.random.fold_in(splits[3], 71), 0)
    pairing = with_ends(jax.random.randint(splits[2], (STEPS, N_COLS), 0, 3), jax.random.fold_in(splits[2], 1), 0, 2).astype(jnp.int32)
    return {"tracks": tracks, "pixel_order": pixel_order, "pairing": pairing}


PAIRINGS = ((0, 1, 2, 3), (0, 2, 1, 3), (0, 3, 1, 2))
UNDOING = ((0, 1, 2, 3), (0, 2, 1, 3), (0, 2, 3, 1))

def rotation(gram_matrix):
    half = gram_matrix.shape[0] // 2
    diagonal = jnp.diagonal(gram_matrix)
    coupling = gram_matrix[:half, half:] / (diagonal[:half, None] + diagonal[None, half:])
    zeros_block = jnp.zeros((half, half), jnp.float32)
    skew_part = jnp.block([[zeros_block, coupling], [-coupling.T, zeros_block]])
    identity = jnp.eye(2 * half, dtype=jnp.float32)
    iterate = (identity + skew_part) / jnp.sqrt(1.0 + jnp.sum(coupling * coupling))
    for count in range(NS_STEPS):
        product = jnp.dot(iterate.T, iterate, precision=lax.Precision.HIGHEST)
        iterate = 1.5 * iterate - 0.5 * jnp.dot(iterate, product, precision=lax.Precision.HIGHEST)
    return iterate

def reference(tracks, pixel_order, pairing):
    residues = NBLK // 2
    shaped = tracks.reshape(BLK, residues, 2, PIXELS)
    matrix = jnp.transpose(shaped, (3, 2, 1, 0)).reshape(PIXELS, NBLK, BLK)
    matrix = jnp.take(matrix, pixel_order.astype(jnp.int32), axis=0)
    table = jnp.array(PAIRINGS, jnp.int32)
    undo_table = jnp.array(UNDOING, jnp.int32)
    for step_index in range(STEPS):
        groups_out = []
        for column_group in range(N_COLS):
            chosen = pairing[step_index, column_group]
            block_set = matrix[:, 4 * column_group:4 * column_group + 4]
            paired = jnp.take(block_set, table[chosen], axis=1).reshape(PIXELS, 2, 2 * BLK)
            turned_pairs = []
            for pair_index in range(2):
                columns = paired[:, pair_index]
                gram_matrix = jnp.dot(columns.T, columns, precision=lax.Precision.HIGHEST)
                turned_pairs.append(jnp.dot(columns, rotation(gram_matrix), precision=lax.Precision.HIGHEST))
            turned = jnp.stack(turned_pairs, axis=1).reshape(PIXELS, 4, BLK)
            groups_out.append(jnp.take(turned, undo_table[chosen], axis=1))
        matrix = jnp.concatenate(groups_out, axis=1)
        if step_index + 1 < STEPS:
            matrix = matrix.at[:, 3::4].set(jnp.roll(matrix[:, 3::4], 1, axis=1))
    matrix = matrix.at[:, 3::4].set(jnp.roll(matrix[:, 3::4], -(STEPS - 1), axis=1))
    return matrix.reshape(PIXELS, NBLK * BLK)
```

```python
import functools

import jax
import jax.numpy as jnp
from jax import lax
from jax.experimental import pallas as pl
from jax.experimental.pallas import tpu as pltpu
from jax.sharding import PartitionSpec as P

STEPS = 2
NS_STEPS = 6
SLOTS = 4
MIB = 1024 * 1024

F32 = jnp.float32
BF16 = jnp.bfloat16
NN = (((1,), (0,)), ((), ()))
NT = (((1,), (1,)), ((), ()))
TN = (((0,), (0,)), ((), ()))


def pair_slots(chosen):
    partner = 2 - chosen
    low = jnp.where(partner == 0, 1, 0)
    high = jnp.where(partner == 2, 1, 2)
    return partner, low, high


def params(mib, flops=0, moved=0):
    return dict(
        compiler_params=pltpu.CompilerParams(vmem_limit_bytes=mib * MIB),
        cost_estimate=pl.CostEstimate(flops=int(flops), bytes_accessed=int(moved), transcendentals=0),
    )


def halves(value):
    high = value.astype(BF16)
    return high, (value - high.astype(F32)).astype(BF16)


def mul(a, b, dims):
    return lax.dot_general(a, b, dims, preferred_element_type=F32)


def dot_split(a, b, dims):
    a_high, a_low = halves(a)
    b_high, b_low = halves(b)
    return mul(a_high, b_high, dims) + (mul(a_high, b_low, dims) + mul(a_low, b_high, dims))


def dot_full(a, b, dims=NN):
    return lax.dot_general(a, b, dims, precision=lax.Precision.HIGHEST, preferred_element_type=F32)


def identity(size):
    return lax.broadcasted_iota(jnp.int32, (size, size), 0) == lax.broadcasted_iota(jnp.int32, (size, size), 1)


LANES = 128
WAYS = 4


def block_rows(refs, slot):
    width = refs[0].shape[0] // SLOTS
    return jnp.concatenate([ref[pl.ds(slot, width, SLOTS), :] for ref in refs], axis=1)


def lane_specs(columns):
    return [pl.BlockSpec((columns, LANES), lambda k, way=way: (0, WAYS * k + way)) for way in range(WAYS)]


def at(ref, row, column, width):
    rows = pl.ds(pl.multiple_of(row * width, width), width)
    columns = pl.ds(pl.multiple_of(column * width, width), width)
    return ref[rows, columns]


def spread_kernel(tracks_ref, pieces_ref):
    frames = tracks_ref.shape[0]
    for component in range(2):
        plane = tracks_ref[:, component, :]
        for group in range(frames // 8):
            for half in range(2):
                pieces_ref[0, 2 * component + half, 4 * group:4 * group + 4, :] = plane[
                    8 * group + 4 * half:8 * group + 4 * half + 4, :]


def spread(tracks, row_devices):
    frames, _, pixels = tracks.shape
    rows = pixels // row_devices
    return pl.pallas_call(
        spread_kernel,
        grid=(row_devices,),
        in_specs=[pl.BlockSpec((frames, 2, rows), lambda r: (0, 0, r))],
        out_specs=pl.BlockSpec((1, 4, frames // 2, rows), lambda r: (r, 0, 0, 0)),
        out_shape=jax.ShapeDtypeStruct((row_devices, 4, frames // 2, rows), F32),
        name="spread",
        **params(16, 0, 8 * tracks.size),
    )(tracks)


def gram_kernel(chosen_ref, *refs):
    held_refs, (sums_ref, gram_ref, last_ref, cross_ref) = refs[:WAYS], refs[WAYS:]
    step = pl.program_id(0)
    width = sums_ref.shape[1]
    high, low = halves(jnp.concatenate([block_rows(held_refs, b) for b in range(SLOTS)], axis=0))
    partner, first, second = pair_slots(chosen_ref[0])
    last_ref[:width, :] = block_rows(held_refs, partner)
    last_ref[width:, :] = block_rows(held_refs, SLOTS - 1)

    @pl.when(step == 0)
    def _():
        gram_ref[...] = jnp.zeros_like(gram_ref)
        cross_ref[...] = jnp.zeros_like(cross_ref)

    gram_ref[...] += mul(high, high, NT)
    cross_ref[...] += mul(high, low, NT)

    @pl.when(step == pl.num_programs(0) - 1)
    def _():
        cross = cross_ref[...]
        gram_ref[...] += cross + cross.T
        sums_ref[:width, :] = at(gram_ref, partner, SLOTS - 1, width)
        sums_ref[width:2 * width, :] = at(gram_ref, first, second, width)
        on_diagonal = identity(width)
        slots = (partner, SLOTS - 1, first, second)
        sums = [jnp.sum(jnp.where(on_diagonal, at(gram_ref, s, s, width), 0.0), axis=0, keepdims=True) for s in slots]
        sums_ref[2 * width:, :] = jnp.concatenate(sums + [jnp.zeros((4, width), F32)], axis=0)


def local_gram(chosen, held):
    columns, rows = held.shape
    width = columns // SLOTS
    chunk = WAYS * LANES
    return pl.pallas_call(
        gram_kernel,
        grid=(rows // chunk,),
        in_specs=[pl.BlockSpec(memory_space=pltpu.SMEM)] + lane_specs(columns),
        out_specs=[
            pl.BlockSpec((2 * width + 8, width), lambda k: (0, 0)),
            pl.BlockSpec((columns, columns), lambda k: (0, 0)),
            pl.BlockSpec((2 * width, chunk), lambda k: (0, k)),
        ],
        out_shape=[
            jax.ShapeDtypeStruct((2 * width + 8, width), F32),
            jax.ShapeDtypeStruct((columns, columns), F32),
            jax.ShapeDtypeStruct((2 * width, rows), F32),
        ],
        scratch_shapes=[pltpu.VMEM((columns, columns), F32)],
        name="gram",
        **params(32, 4 * columns * columns * rows, 6 * held.size),
    )(chosen, *[held] * WAYS)


def cross_kernel(chosen_ref, *refs):
    held_refs, (came_ref, cross_ref, own_ref) = refs[:WAYS], refs[WAYS:]
    step = pl.program_id(0)
    partner, first, second = pair_slots(chosen_ref[0])
    meets = 2 - chosen_ref[1]
    in_last = meets == partner
    one = jnp.where(in_last, partner, first)
    two = jnp.where(in_last, SLOTS - 1, second)
    here = jnp.concatenate([block_rows(held_refs, s) for s in (one, two)], axis=0)
    here_high, here_low = halves(here)
    came_high, came_low = halves(came_ref[...])
    cross = mul(here_high, came_high, NT) + (mul(here_high, came_low, NT) + mul(here_low, came_high, NT))
    twice = mul(came_high, came_low, NT)
    own = mul(came_high, came_high, NT) + (twice + twice.T)

    @pl.when(step == 0)
    def _():
        cross_ref[...] = cross
        own_ref[...] = own

    @pl.when(step > 0)
    def _():
        cross_ref[...] += cross
        own_ref[...] += own


def cross_gram(chosen, held, came):
    columns, rows = held.shape
    pair = came.shape[0]
    chunk = WAYS * LANES
    square = jax.ShapeDtypeStruct((pair, pair), F32)
    return pl.pallas_call(
        cross_kernel,
        grid=(rows // chunk,),
        in_specs=[pl.BlockSpec(memory_space=pltpu.SMEM)] + lane_specs(columns) + [
            pl.BlockSpec((pair, chunk), lambda k: (0, k))],
        out_specs=[pl.BlockSpec((pair, pair), lambda k: (0, 0))] * 2,
        out_shape=[square, square],
        name="cross_gram",
        **params(32, 10 * pair * pair * rows, 6 * held.size),
    )(chosen, *[held] * WAYS, came)


def rotations(grams):
    width = grams[0][0].shape[0]
    eye = identity(width).astype(F32)
    couplings, scales, squares, products = [], [], [], []
    for block, row_sums, column_sums in grams:
        spread_sums = jnp.broadcast_to(row_sums, (width, width)).T
        coupling = block / (spread_sums + column_sums)
        total = 1.0 + jnp.sum(coupling * coupling)
        couplings.append(coupling)
        for dims in (NT, TN):
            scales.append(1.0 / jnp.sqrt(total))
            squares.append((eye + dot_full(coupling, coupling, dims)) / total)
    for count in range(NS_STEPS):
        factors = [1.5 * eye - 0.5 * square for square in squares]
        if count == 0:
            products = [scale * factor for scale, factor in zip(scales, factors)]
        else:
            products = [dot_full(product, factor) for product, factor in zip(products, factors)]
        if count + 1 < NS_STEPS:
            squares = [dot_full(square, factor) for square, factor in zip(squares, factors)]
            squares = [dot_full(square, factor) for square, factor in zip(squares, factors)]
    results = []
    for index, coupling in enumerate(couplings):
        across = dot_full(products[2 * index], coupling)
        results.append((products[2 * index], across, -across.T, products[2 * index + 1]))
    return results


def rotation_kernel(sums_ref, came_ref, rotation_ref):
    width = sums_ref.shape[1]
    sums = sums_ref[2 * width:, :]
    came = came_ref[width:, :]
    grams = [
        (sums_ref[:width, :], sums[0:1], sums[1:2]),
        (sums_ref[width:2 * width, :], sums[2:3], sums[3:4]),
        (came_ref[:width, :], came[0:1], came[1:2]),
    ]
    for index, (top, right, bottom, end) in enumerate(rotations(grams)):
        rotation_ref[index, :width, :width] = top
        rotation_ref[index, :width, width:] = right
        rotation_ref[index, width:, :width] = bottom
        rotation_ref[index, width:, width:] = end


def three_rotations(sums, came):
    width = sums.shape[1]
    return pl.pallas_call(
        rotation_kernel,
        out_shape=jax.ShapeDtypeStruct((3, 2 * width, 2 * width), F32),
        name="rotations",
        **params(16, 200 * 6 * width**3, 16 * width * width),
    )(sums, came)


def second_kernel(chosen_ref, gram_ref, cross_ref, own_ref, rotation_ref, sums_ref):
    width = sums_ref.shape[1]
    partner, first, second = pair_slots(chosen_ref[0])
    meets, low, high = pair_slots(chosen_ref[1])

    def place(slot):
        in_last = slot == partner
        members = (jnp.where(in_last, partner, first), jnp.where(in_last, SLOTS - 1, second))
        columns = jnp.where(jnp.logical_or(in_last, slot == first), 0, 1)
        turn = rotation_ref[jnp.where(in_last, 0, 1), :, pl.ds(pl.multiple_of(columns * width, width), width)]
        return members, turn

    def between(rows, columns):
        return jnp.concatenate(
            [jnp.concatenate([at(gram_ref, r, c, width) for c in columns], axis=1) for r in rows], axis=0)

    (meets_in, meets_turn), (low_in, low_turn), (high_in, high_turn) = place(meets), place(low), place(high)
    came_turn = rotation_ref[2, :, width:]
    sums_ref[:width, :] = dot_split(meets_turn, dot_split(cross_ref[...], came_turn, NN), TN)
    sums_ref[width:2 * width, :] = dot_split(low_turn, dot_split(between(low_in, high_in), high_turn, NN), TN)

    def squares(gram, turn):
        return jnp.sum(turn * dot_split(gram, turn, NN), axis=0, keepdims=True)

    rows = [
        squares(between(meets_in, meets_in), meets_turn),
        squares(own_ref[...], came_turn),
        squares(between(low_in, low_in), low_turn),
        squares(between(high_in, high_in), high_turn),
        jnp.zeros((4, width), F32),
    ]
    sums_ref[2 * width:, :] = jnp.concatenate(rows, axis=0)


def second_sums(chosen, gram, cross, own, turns):
    width = gram.shape[0] // SLOTS
    vmem = pl.BlockSpec(memory_space=pltpu.VMEM)
    return pl.pallas_call(
        second_kernel,
        in_specs=[pl.BlockSpec(memory_space=pltpu.SMEM)] + [vmem] * 4,
        out_specs=vmem,
        out_shape=jax.ShapeDtypeStruct((2 * width + 8, width), F32),
        name="second_sums",
        **params(16, 6 * 32 * width**3, 16 * gram.size),
    )(chosen, gram, cross, own, turns)


def picks(order_ref, rows):
    order = order_ref[...]
    return jnp.where(lax.broadcasted_iota(jnp.int32, (rows, order.shape[1]), 0) == order, 1.0, 0.0).astype(BF16)


def order_kernel(order_ref, held_ref, matrix_ref, split_ref, turned_ref):
    columns, rows = held_ref.shape
    width = columns // SLOTS

    @pl.when(pl.program_id(0) == 0)
    def _():
        high, low = halves(held_ref[...])
        split_ref[:columns, :] = high
        split_ref[columns:, :] = low

    both = mul(split_ref[...], picks(order_ref, rows), NN)
    both = both[:columns] + both[columns:]
    for part in range(matrix_ref.shape[1] // LANES):
        lanes = slice(part * LANES, (part + 1) * LANES)
        turned_ref[part] = both[:, lanes]
        for block in range(SLOTS):
            matrix_ref[block, lanes, :] = turned_ref[part, pl.ds(block, width, SLOTS), :].T


def ordered(order, held):
    columns, rows = held.shape
    width = columns // SLOTS
    chunk = 2 * width
    return pl.pallas_call(
        order_kernel,
        grid=(rows // chunk,),
        in_specs=[
            pl.BlockSpec((1, chunk), lambda k: (0, k)),
            pl.BlockSpec((columns, rows), lambda k: (0, 0)),
        ],
        out_specs=pl.BlockSpec((SLOTS, chunk, width), lambda k: (0, k, 0)),
        out_shape=jax.ShapeDtypeStruct((SLOTS, rows, width), F32),
        scratch_shapes=[pltpu.VMEM((2 * columns, rows), BF16), pltpu.VMEM((chunk // LANES, columns, LANES), F32)],
        name="row_order",
        **params(40, 4 * columns * rows * rows, 8 * held.size),
    )(order, held)


def turn_kernel(chosen_ref, matrix_ref, rotation_ref, turned_ref, meets_ref):
    width = matrix_ref.shape[2]
    partner, first, second = pair_slots(chosen_ref[0])
    for index, (one, two) in enumerate(((partner, SLOTS - 1), (first, second))):
        pair = jnp.concatenate([matrix_ref[one], matrix_ref[two]], axis=1)
        turned = dot_split(pair, rotation_ref[index], NN)
        turned_ref[one] = turned[:, :width]
        turned_ref[two] = turned[:, width:]
    meets_ref[...] = turned_ref[2 - chosen_ref[1]]


def turn(chosen, matrix, turns):
    _, rows, width = matrix.shape
    chunk = rows // 4
    return pl.pallas_call(
        turn_kernel,
        grid=(rows // chunk,),
        in_specs=[
            pl.BlockSpec(memory_space=pltpu.SMEM),
            pl.BlockSpec((SLOTS, chunk, width), lambda k: (0, k, 0)),
            pl.BlockSpec(turns.shape, lambda k: (0, 0, 0)),
        ],
        out_specs=[
            pl.BlockSpec((SLOTS, chunk, width), lambda k: (0, k, 0)),
            pl.BlockSpec((chunk, width), lambda k: (k, 0)),
        ],
        out_shape=[jax.ShapeDtypeStruct(matrix.shape, F32), jax.ShapeDtypeStruct((rows, width), F32)],
        name="first_turn",
        **params(32, 24 * rows * width * width, 9 * matrix.size),
    )(chosen, matrix, turns)


def moved_kernel(order_ref, came_ref, rotation_ref, block_ref, split_ref):
    width = block_ref.shape[1]
    rows = came_ref.shape[1]

    @pl.when(pl.program_id(0) == 0)
    def _():
        high, low = halves(dot_split(rotation_ref[2, :, width:], came_ref[...], TN))
        split_ref[:width, :] = high
        split_ref[width:, :] = low

    both = mul(split_ref[...], picks(order_ref, rows), NN)
    block_ref[...] = (both[:width] + both[width:]).T


def moved_block(order, came, turns):
    pair, rows = came.shape
    width = pair // 2
    chunk = pair
    return pl.pallas_call(
        moved_kernel,
        grid=(rows // chunk,),
        in_specs=[
            pl.BlockSpec((1, chunk), lambda k: (0, k)),
            pl.BlockSpec((pair, rows), lambda k: (0, 0)),
            pl.BlockSpec(turns.shape, lambda k: (0, 0, 0)),
        ],
        out_specs=pl.BlockSpec((chunk, width), lambda k: (k, 0)),
        out_shape=jax.ShapeDtypeStruct((rows, width), F32),
        scratch_shapes=[pltpu.VMEM((pair, rows), BF16)],
        name="moved_block",
        **params(32, 4 * width * rows * rows, 8 * came.size),
    )(order, came, turns)


def finish_kernel(chosen_ref, turned_ref, moved_ref, behind_ref, rotation_ref, out_ref):
    width = moved_ref.shape[1]
    meets, low, high = pair_slots(chosen_ref[1])

    def put(slot, value):
        out_ref[:, pl.ds(pl.multiple_of(slot * width, width), width)] = value

    pair = dot_split(jnp.concatenate([turned_ref[low], turned_ref[high]], axis=1), rotation_ref[1], NN)
    put(low, pair[:, :width])
    put(high, pair[:, width:])
    put(meets, dot_split(
        jnp.concatenate([turned_ref[meets], moved_ref[...]], axis=1), rotation_ref[0, :, :width], NN))
    put(SLOTS - 1, dot_split(
        jnp.concatenate([behind_ref[...], turned_ref[SLOTS - 1]], axis=1), rotation_ref[2, :, width:], NN))


def finish(chosen, turned, moved, behind, turns):
    _, rows, width = turned.shape
    chunk = rows // 4
    block = pl.BlockSpec((chunk, width), lambda k: (k, 0))
    return pl.pallas_call(
        finish_kernel,
        grid=(rows // chunk,),
        in_specs=[
            pl.BlockSpec(memory_space=pltpu.SMEM),
            pl.BlockSpec((SLOTS, chunk, width), lambda k: (0, k, 0)),
            block,
            block,
            pl.BlockSpec(turns.shape, lambda k: (0, 0, 0)),
        ],
        out_specs=pl.BlockSpec((chunk, SLOTS * width), lambda k: (k, 0)),
        out_shape=jax.ShapeDtypeStruct((rows, SLOTS * width), F32),
        name="second_turn",
        **params(32, 24 * rows * width * width, 10 * turned.size),
    )(chosen, turned, moved, behind, turns)


def from_behind(value, axis, steps):
    count = lax.axis_size(axis)
    pairs = [(source, (source + steps) % count) for source in range(count)]
    return lax.ppermute(value, axis, pairs)


def summed(value, axis):
    count = lax.axis_size(axis)
    if count & (count - 1):
        return lax.psum(value, axis)
    distance = 1
    while distance < count:
        pairs = [(source, source ^ distance) for source in range(count)]
        value = value + lax.ppermute(value, axis, pairs)
        distance *= 2
    return value


def last_pair(sums):
    width = sums.shape[1]
    return jnp.concatenate([sums[:width], sums[2 * width:]], axis=0)


def body(tracks, pixel_order, pairing):
    frames_dev, _, pixel_total = tracks.shape
    row_devices = lax.axis_size("rows")
    row_count = pixel_total // row_devices
    pieces = spread(tracks, row_devices).reshape(row_devices * 4, frames_dev // 2, row_count)
    arrived = lax.all_to_all(pieces, ("rows", "cols"), split_axis=0, concat_axis=0, tiled=True)
    held = arrived.reshape(-1, row_count)
    order = (pixel_order - lax.axis_index("rows") * row_count).reshape(1, row_count)
    chosen = lax.dynamic_index_in_dim(pairing, lax.axis_index("cols"), axis=1, keepdims=False)

    sums, gram, last = local_gram(chosen, held)
    came = from_behind(last, "cols", 1)
    sums = summed(sums, "rows")
    matrix = ordered(order, held)
    came_sums = from_behind(last_pair(sums), "cols", 1)
    turns = three_rotations(sums, came_sums)
    cross, own = cross_gram(chosen, held, came)

    sums = summed(second_sums(chosen, gram, cross, own, turns), "rows")
    turned, meets = turn(chosen, matrix, turns)
    behind = from_behind(meets, "cols", -1)
    moved = moved_block(order, came, turns)
    behind_sums = from_behind(last_pair(sums), "cols", -1)
    turns = three_rotations(sums, behind_sums)
    return finish(chosen, turned, moved, behind, turns)


def solution(mesh):
    placed = (P(("rows", "cols"), None, None), P("rows"), P())
    return jax.shard_map(
        body, mesh=mesh, in_specs=placed, out_specs=P("rows", "cols"), check_vma=False
    )
```

```python
import jax
import jax.numpy as jnp
from jax import lax
from jax.experimental import pallas as pl
from jax.experimental.pallas import tpu as pltpu
from jax.sharding import PartitionSpec as P

STEPS = 2
NS_STEPS = 6
SLOTS = 4
MIB = 1024 * 1024

F32 = jnp.float32
BF16 = jnp.bfloat16
NN = (((1,), (0,)), ((), ()))
NT = (((1,), (1,)), ((), ()))
TN = (((0,), (0,)), ((), ()))


def pair_slots(chosen):
    partner = 2 - chosen
    low = jnp.where(partner == 0, 1, 0)
    high = jnp.where(partner == 2, 1, 2)
    return partner, low, high


def params(mib, flops=0, moved=0):
    return dict(
        compiler_params=pltpu.CompilerParams(vmem_limit_bytes=mib * MIB),
        cost_estimate=pl.CostEstimate(flops=int(flops), bytes_accessed=int(moved), transcendentals=0),
    )


def halves(value):
    high = value.astype(BF16)
    return high, (value - high.astype(F32)).astype(BF16)


def mul(a, b, dims):
    return lax.dot_general(a, b, dims, preferred_element_type=F32)


def dot_split(a, b, dims):
    a_high, a_low = halves(a)
    b_high, b_low = halves(b)
    return mul(a_high, b_high, dims) + (mul(a_high, b_low, dims) + mul(a_low, b_high, dims))


def dot_full(a, b, dims=NN):
    return lax.dot_general(a, b, dims, precision=lax.Precision.HIGHEST, preferred_element_type=F32)


def identity(size):
    return lax.broadcasted_iota(jnp.int32, (size, size), 0) == lax.broadcasted_iota(jnp.int32, (size, size), 1)


LANES = 128
WAYS = 8


def block_rows(refs, slot):
    width = refs[0].shape[0] // SLOTS
    return jnp.concatenate([ref[pl.ds(slot, width, SLOTS), :] for ref in refs], axis=1)


def lane_specs(columns):
    return [pl.BlockSpec((columns, LANES), lambda k, way=way: (0, WAYS * k + way)) for way in range(WAYS)]


def at(ref, row, column, width):
    rows = pl.ds(pl.multiple_of(row * width, width), width)
    columns = pl.ds(pl.multiple_of(column * width, width), width)
    return ref[rows, columns]


def spread_kernel(tracks_ref, pieces_ref, came_ref, ready_ref, in_sems, out_sems):
    row_devices, frames, _, rows = came_ref.shape
    loads = [
        pltpu.make_async_copy(tracks_ref.at[:, :, pl.ds(r * rows, rows)], came_ref.at[r], in_sems.at[r])
        for r in range(row_devices)
    ]
    stores = [
        pltpu.make_async_copy(ready_ref.at[r], pieces_ref.at[r], out_sems.at[r]) for r in range(row_devices)
    ]
    for load in loads:
        load.start()
    for r in range(row_devices):
        loads[r].wait()
        for component in range(2):
            plane = came_ref[r, :, component, :]
            for group in range(frames // 8):
                for half in range(2):
                    ready_ref[r, 2 * component + half, 4 * group:4 * group + 4, :] = plane[
                        8 * group + 4 * half:8 * group + 4 * half + 4, :]
        stores[r].start()
    for store in stores:
        store.wait()


def spread(tracks, row_devices):
    frames, _, pixels = tracks.shape
    rows = pixels // row_devices
    shape = (row_devices, 4, frames // 2, rows)
    return pl.pallas_call(
        spread_kernel,
        in_specs=[pl.BlockSpec(memory_space=pl.ANY)],
        out_specs=pl.BlockSpec(memory_space=pl.ANY),
        out_shape=jax.ShapeDtypeStruct(shape, F32),
        scratch_shapes=[
            pltpu.VMEM((row_devices, frames, 2, rows), F32),
            pltpu.VMEM(shape, F32),
            pltpu.SemaphoreType.DMA((row_devices,)),
            pltpu.SemaphoreType.DMA((row_devices,)),
        ],
        name="spread",
        **params(48, 0, 8 * tracks.size),
    )(tracks)


def coupling_kernel(chosen_ref, *refs):
    held_refs, (sums_ref, last_ref, products_ref, squares_ref) = refs[:WAYS], refs[WAYS:]
    step = pl.program_id(0)
    width = sums_ref.shape[1]
    partner, first, second = pair_slots(chosen_ref[0])

    @pl.when(step == 0)
    def _():
        products_ref[...] = jnp.zeros_like(products_ref)
        squares_ref[...] = jnp.zeros_like(squares_ref)

    for index, slots in enumerate(((partner, SLOTS - 1), (first, second))):
        both = []
        for side, slot in enumerate(slots):
            block = block_rows(held_refs, slot)
            if index == 0:
                last_ref[side * width:(side + 1) * width, :] = block
            squared = block * block
            folded = squared[:, :LANES]
            for way in range(1, WAYS):
                folded += squared[:, way * LANES:(way + 1) * LANES]
            squares_ref[2 * index + side] += folded
            both.append(jnp.concatenate(halves(block), axis=0))
        products_ref[index] += mul(both[0], both[1], NT)

    @pl.when(step == pl.num_programs(0) - 1)
    def _():
        for index in range(2):
            product = products_ref[index]
            top = product[:width, :width] + (product[:width, width:] + product[width:, :width])
            sums_ref[index * width:(index + 1) * width, :] = top + product[width:, width:]
        rows = [jnp.sum(squares_ref[slot].T, axis=0, keepdims=True) for slot in range(SLOTS)]
        sums_ref[2 * width:, :] = jnp.concatenate(rows + [jnp.zeros((4, width), F32)], axis=0)


def couplings(chosen, held):
    columns, rows = held.shape
    width = columns // SLOTS
    chunk = WAYS * LANES
    return pl.pallas_call(
        coupling_kernel,
        grid=(rows // chunk,),
        in_specs=[pl.BlockSpec(memory_space=pltpu.SMEM)] + lane_specs(columns),
        out_specs=[
            pl.BlockSpec((2 * width + 8, width), lambda k: (0, 0)),
            pl.BlockSpec((2 * width, chunk), lambda k: (0, k)),
        ],
        out_shape=[
            jax.ShapeDtypeStruct((2 * width + 8, width), F32),
            jax.ShapeDtypeStruct((2 * width, rows), F32),
        ],
        scratch_shapes=[
            pltpu.VMEM((2, 2 * width, 2 * width), F32),
            pltpu.VMEM((SLOTS, width, LANES), F32),
        ],
        name="couplings",
        **params(24, 16 * width * width * rows, 6 * held.size),
    )(chosen, *[held] * WAYS)


def gram_kernel(*refs):
    held_refs, (_, gram_ref, split_ref, cross_ref) = refs[:WAYS], refs[WAYS:]
    step = pl.program_id(0)
    columns = gram_ref.shape[0]
    high, low = halves(jnp.concatenate([block_rows(held_refs, b) for b in range(SLOTS)], axis=0))
    split_ref[:columns, :] = high
    split_ref[columns:, :] = low

    @pl.when(step == 0)
    def _():
        gram_ref[...] = mul(high, high, NT)
        cross_ref[...] = mul(high, low, NT)

    @pl.when(step > 0)
    def _():
        gram_ref[...] += mul(high, high, NT)
        cross_ref[...] += mul(high, low, NT)

    @pl.when(step == pl.num_programs(0) - 1)
    def _():
        cross = cross_ref[...]
        gram_ref[...] += cross + cross.T


def local_gram(held, after):
    columns, rows = held.shape
    chunk = WAYS * LANES
    return pl.pallas_call(
        gram_kernel,
        grid=(rows // chunk,),
        in_specs=lane_specs(columns) + [pl.BlockSpec(memory_space=pl.ANY)],
        out_specs=[
            pl.BlockSpec((columns, columns), lambda k: (0, 0)),
            pl.BlockSpec((2 * columns, chunk), lambda k: (0, k)),
        ],
        out_shape=[
            jax.ShapeDtypeStruct((columns, columns), F32),
            jax.ShapeDtypeStruct((2 * columns, rows), BF16),
        ],
        scratch_shapes=[pltpu.VMEM((columns, columns), F32)],
        name="gram",
        **params(32, 4 * columns * columns * rows, 8 * held.size),
    )(*[held] * WAYS, after)


def cross_kernel(chosen_ref, split_ref, came_ref, _, cross_ref, own_ref):
    width = came_ref.shape[0] // 2
    columns = split_ref.shape[0] // 2
    partner, first, second = pair_slots(chosen_ref[0])
    in_last = 2 - chosen_ref[1] == partner
    members = (jnp.where(in_last, partner, first), jnp.where(in_last, SLOTS - 1, second))
    here_high, here_low = [
        jnp.concatenate(
            [split_ref[pl.ds(pl.multiple_of(start + m * width, width), width), :] for m in members], axis=0)
        for start in (0, columns)
    ]
    came_high, came_low = halves(came_ref[...])
    cross_ref[...] = mul(here_high, came_high, NT) + (mul(here_high, came_low, NT) + mul(here_low, came_high, NT))
    twice = mul(came_high, came_low, NT)
    own_ref[...] = mul(came_high, came_high, NT) + (twice + twice.T)


def cross_gram(chosen, split, came, after):
    pair, rows = came.shape
    vmem = pl.BlockSpec(memory_space=pltpu.VMEM)
    square = jax.ShapeDtypeStruct((pair, pair), F32)
    return pl.pallas_call(
        cross_kernel,
        in_specs=[pl.BlockSpec(memory_space=pltpu.SMEM), vmem, vmem, pl.BlockSpec(memory_space=pl.ANY)],
        out_specs=[vmem, vmem],
        out_shape=[square, square],
        name="cross_gram",
        **params(24, 10 * pair * pair * rows, 8 * came.size),
    )(chosen, split, came, after)


def rotations(grams):
    width = grams[0][0].shape[0]
    eye = identity(width).astype(F32)
    couplings, scales, squares, products = [], [], [], []
    for block, row_sums, column_sums in grams:
        spread_sums = jnp.broadcast_to(row_sums, (width, width)).T
        coupling = block / (spread_sums + column_sums)
        total = 1.0 + jnp.sum(coupling * coupling)
        couplings.append(coupling)
        for dims in (NT, TN):
            scales.append(1.0 / jnp.sqrt(total))
            squares.append((eye + dot_full(coupling, coupling, dims)) / total)
    for count in range(NS_STEPS):
        factors = [1.5 * eye - 0.5 * square for square in squares]
        if count == 0:
            products = [scale * factor for scale, factor in zip(scales, factors)]
        else:
            products = [dot_full(product, factor) for product, factor in zip(products, factors)]
        if count + 1 < NS_STEPS:
            squares = [dot_full(square, factor) for square, factor in zip(squares, factors)]
            squares = [dot_full(square, factor) for square, factor in zip(squares, factors)]
    results = []
    for index, coupling in enumerate(couplings):
        across = dot_full(products[2 * index], coupling)
        results.append((products[2 * index], across, -across.T, products[2 * index + 1]))
    return results


def rotation_kernel(sums_ref, came_ref, *refs):
    rotation_ref = refs[-1]
    width = sums_ref.shape[1]
    sums = sums_ref[2 * width:, :]
    came = came_ref[width:, :]
    grams = [
        (sums_ref[:width, :], sums[0:1], sums[1:2]),
        (sums_ref[width:2 * width, :], sums[2:3], sums[3:4]),
        (came_ref[:width, :], came[0:1], came[1:2]),
    ]
    for index, (top, right, bottom, end) in enumerate(rotations(grams)):
        rotation_ref[index, :width, :width] = top
        rotation_ref[index, :width, width:] = right
        rotation_ref[index, width:, :width] = bottom
        rotation_ref[index, width:, width:] = end


def three_rotations(sums, came, *after):
    width = sums.shape[1]
    vmem = pl.BlockSpec(memory_space=pltpu.VMEM)
    return pl.pallas_call(
        rotation_kernel,
        in_specs=[vmem, vmem] + [pl.BlockSpec(memory_space=pl.ANY)] * len(after),
        out_specs=vmem,
        out_shape=jax.ShapeDtypeStruct((3, 2 * width, 2 * width), F32),
        name="rotations",
        **params(16, 200 * 6 * width**3, 16 * width * width),
    )(sums, came, *after)


def second_kernel(chosen_ref, gram_ref, cross_ref, own_ref, rotation_ref, sums_ref):
    width = sums_ref.shape[1]
    partner, first, second = pair_slots(chosen_ref[0])
    meets, low, high = pair_slots(chosen_ref[1])

    def place(slot):
        in_last = slot == partner
        members = (jnp.where(in_last, partner, first), jnp.where(in_last, SLOTS - 1, second))
        columns = jnp.where(jnp.logical_or(in_last, slot == first), 0, 1)
        turn = rotation_ref[jnp.where(in_last, 0, 1), :, pl.ds(pl.multiple_of(columns * width, width), width)]
        return members, turn

    def between(rows, columns):
        return jnp.concatenate(
            [jnp.concatenate([at(gram_ref, r, c, width) for c in columns], axis=1) for r in rows], axis=0)

    (meets_in, meets_turn), (low_in, low_turn), (high_in, high_turn) = place(meets), place(low), place(high)
    came_turn = rotation_ref[2, :, width:]
    sums_ref[:width, :] = dot_split(meets_turn, dot_split(cross_ref[...], came_turn, NN), TN)
    sums_ref[width:2 * width, :] = dot_split(low_turn, dot_split(between(low_in, high_in), high_turn, NN), TN)

    def squares(gram, turn):
        return jnp.sum(turn * dot_split(gram, turn, NN), axis=0, keepdims=True)

    rows = [
        squares(between(meets_in, meets_in), meets_turn),
        squares(own_ref[...], came_turn),
        squares(between(low_in, low_in), low_turn),
        squares(between(high_in, high_in), high_turn),
        jnp.zeros((4, width), F32),
    ]
    sums_ref[2 * width:, :] = jnp.concatenate(rows, axis=0)


def second_sums(chosen, gram, cross, own, turns):
    width = gram.shape[0] // SLOTS
    vmem = pl.BlockSpec(memory_space=pltpu.VMEM)
    return pl.pallas_call(
        second_kernel,
        in_specs=[pl.BlockSpec(memory_space=pltpu.SMEM)] + [vmem] * 4,
        out_specs=vmem,
        out_shape=jax.ShapeDtypeStruct((2 * width + 8, width), F32),
        name="second_sums",
        **params(16, 6 * 32 * width**3, 16 * gram.size),
    )(chosen, gram, cross, own, turns)


def picks(order_ref, rows):
    order = order_ref[...]
    return jnp.where(lax.broadcasted_iota(jnp.int32, (rows, order.shape[1]), 0) == order, 1.0, 0.0).astype(BF16)


def order_kernel(order_ref, split_ref, *refs):
    matrix_ref = refs[-1]
    rows = split_ref.shape[1]
    width = matrix_ref.shape[2]
    columns = SLOTS * width
    both = mul(split_ref[...], picks(order_ref, rows), NN)
    both = both[:columns] + both[columns:]
    for block in range(SLOTS):
        matrix_ref[block] = both[block * width:(block + 1) * width].T


def ordered(order, split, after, tiles, into=None):
    columns, rows = split.shape[0] // 2, split.shape[1]
    width = columns // SLOTS
    chunk = 2 * width
    start, stop = tiles
    extra = (after,) if into is None else (after, into)
    return pl.pallas_call(
        order_kernel,
        grid=(stop - start,),
        in_specs=[
            pl.BlockSpec((1, chunk), lambda k: (0, k + start)),
            pl.BlockSpec((2 * columns, rows), lambda k: (0, 0)),
        ] + [pl.BlockSpec(memory_space=pl.ANY)] * len(extra),
        out_specs=pl.BlockSpec((SLOTS, chunk, width), lambda k: (0, k + start, 0)),
        out_shape=jax.ShapeDtypeStruct((SLOTS, rows, width), F32),
        input_output_aliases={} if into is None else {3: 0},
        name="row_order",
        **params(32, 4 * columns * rows * chunk * (stop - start), 8 * columns * rows),
    )(order, split, *extra)


def turn_kernel(chosen_ref, matrix_ref, rotation_ref, _, turned_ref, meets_ref):
    width = matrix_ref.shape[2]
    partner, first, second = pair_slots(chosen_ref[0])
    for index, (one, two) in enumerate(((partner, SLOTS - 1), (first, second))):
        pair = jnp.concatenate([matrix_ref[one], matrix_ref[two]], axis=1)
        turned = dot_split(pair, rotation_ref[index], NN)
        turned_ref[one] = turned[:, :width]
        turned_ref[two] = turned[:, width:]
    meets_ref[...] = turned_ref[2 - chosen_ref[1]]


def turn(chosen, matrix, turns, after):
    _, rows, width = matrix.shape
    chunk = rows // 2
    return pl.pallas_call(
        turn_kernel,
        grid=(rows // chunk,),
        in_specs=[
            pl.BlockSpec(memory_space=pltpu.SMEM),
            pl.BlockSpec((SLOTS, chunk, width), lambda k: (0, k, 0)),
            pl.BlockSpec(turns.shape, lambda k: (0, 0, 0)),
            pl.BlockSpec(memory_space=pl.ANY),
        ],
        out_specs=[
            pl.BlockSpec((SLOTS, chunk, width), lambda k: (0, k, 0)),
            pl.BlockSpec((chunk, width), lambda k: (k, 0)),
        ],
        out_shape=[jax.ShapeDtypeStruct(matrix.shape, F32), jax.ShapeDtypeStruct((rows, width), F32)],
        name="first_turn",
        **params(32, 24 * rows * width * width, 9 * matrix.size),
    )(chosen, matrix, turns, after)


def moved_kernel(order_ref, came_ref, rotation_ref, _, block_ref, split_ref):
    width = block_ref.shape[1]
    rows = came_ref.shape[1]

    @pl.when(pl.program_id(0) == 0)
    def _():
        high, low = halves(dot_split(rotation_ref[2, :, width:], came_ref[...], TN))
        split_ref[:width, :] = high
        split_ref[width:, :] = low

    both = mul(split_ref[...], picks(order_ref, rows), NN)
    block_ref[...] = (both[:width] + both[width:]).T


def moved_block(order, came, turns, after):
    pair, rows = came.shape
    width = pair // 2
    chunk = pair
    return pl.pallas_call(
        moved_kernel,
        grid=(rows // chunk,),
        in_specs=[
            pl.BlockSpec((1, chunk), lambda k: (0, k)),
            pl.BlockSpec((pair, rows), lambda k: (0, 0)),
            pl.BlockSpec(turns.shape, lambda k: (0, 0, 0)),
            pl.BlockSpec(memory_space=pl.ANY),
        ],
        out_specs=pl.BlockSpec((chunk, width), lambda k: (k, 0)),
        out_shape=jax.ShapeDtypeStruct((rows, width), F32),
        scratch_shapes=[pltpu.VMEM((pair, rows), BF16)],
        name="moved_block",
        **params(32, 4 * width * rows * rows, 8 * came.size),
    )(order, came, turns, after)


PARTS = 4


def finish_kernel(chosen_ref, turned_ref, moved_ref, behind_ref, rotation_ref, out_ref, ready_ref, sems):
    rows, width = moved_ref.shape
    meets, low, high = pair_slots(chosen_ref[1])
    chunk = rows // PARTS
    stores = []
    for part in range(PARTS):
        here = pl.ds(part * chunk, chunk)

        def put(slot, value, here=here):
            ready_ref[here, pl.ds(pl.multiple_of(slot * width, width), width)] = value

        pair = dot_split(jnp.concatenate([turned_ref[low, here], turned_ref[high, here]], axis=1), rotation_ref[1], NN)
        put(low, pair[:, :width])
        put(high, pair[:, width:])
        put(meets, dot_split(
            jnp.concatenate([turned_ref[meets, here], moved_ref[here]], axis=1), rotation_ref[0, :, :width], NN))
        put(SLOTS - 1, dot_split(
            jnp.concatenate([behind_ref[here], turned_ref[SLOTS - 1, here]], axis=1), rotation_ref[2, :, width:], NN))
        stores.append(pltpu.make_async_copy(ready_ref.at[here], out_ref.at[here], sems.at[part]))
        stores[-1].start()
    for store in stores:
        store.wait()


def finish(chosen, turned, moved, behind, turns):
    _, rows, width = turned.shape
    vmem = pl.BlockSpec(memory_space=pltpu.VMEM)
    return pl.pallas_call(
        finish_kernel,
        in_specs=[pl.BlockSpec(memory_space=pltpu.SMEM)] + [vmem] * 4,
        out_specs=pl.BlockSpec(memory_space=pl.ANY),
        out_shape=jax.ShapeDtypeStruct((rows, SLOTS * width), F32),
        scratch_shapes=[pltpu.VMEM((rows, SLOTS * width), F32), pltpu.SemaphoreType.DMA((PARTS,))],
        name="second_turn",
        **params(32, 24 * rows * width * width, 10 * turned.size),
    )(chosen, turned, moved, behind, turns)


def add_kernel(one_ref, two_ref, *refs):
    total_ref, last_ref = refs[-2:]
    width = one_ref.shape[1]
    total = one_ref[...] + two_ref[...]
    total_ref[...] = total
    last_ref[:width] = total[:width]
    last_ref[width:] = total[2 * width:]


def added(one, two, after):
    height, width = one.shape
    vmem = pl.BlockSpec(memory_space=pltpu.VMEM)
    return pl.pallas_call(
        add_kernel,
        in_specs=[vmem, vmem] + [pl.BlockSpec(memory_space=pl.ANY)] * len(after),
        out_specs=[vmem, vmem],
        out_shape=[jax.ShapeDtypeStruct(one.shape, F32), jax.ShapeDtypeStruct((height - width, width), F32)],
        name="add",
        **params(8, one.size, 16 * one.size),
    )(one, two, *after)


def from_behind(value, axis, steps):
    count = lax.axis_size(axis)
    pairs = [(source, (source + steps) % count) for source in range(count)]
    return lax.ppermute(value, axis, pairs)


def summed(value, axis, beside):
    count = lax.axis_size(axis)
    width = value.shape[1]
    last = None
    distance = 1
    while distance < count:
        if count & (count - 1):
            value, distance = lax.psum(value, axis), count
            break
        got = lax.ppermute(value, axis, [(source, source ^ distance) for source in range(count)])
        after = beside.pop(0)(value) if beside else ()
        value, last = added(value, got, after)
        distance *= 2
    for work in beside:
        work(value)
    if last is None:
        last = jnp.concatenate([value[:width], value[2 * width:]], axis=0)
    return value, last


def body(tracks, pixel_order, pairing):
    frames_dev, _, pixel_total = tracks.shape
    row_devices = lax.axis_size("rows")
    row_count = pixel_total // row_devices
    pieces = spread(tracks, row_devices).reshape(row_devices * 4, frames_dev // 2, row_count)
    arrived = lax.all_to_all(pieces, ("rows", "cols"), split_axis=0, concat_axis=0, tiled=True)
    held = arrived.reshape(-1, row_count)
    order = (pixel_order - lax.axis_index("rows") * row_count).reshape(1, row_count)
    chosen = lax.dynamic_index_in_dim(pairing, lax.axis_index("cols"), axis=1, keepdims=False)
    tiles = row_count // (held.shape[0] // 2)
    kept = {}

    def gram_work(after):
        kept["gram"], kept["split"] = local_gram(held, after)
        return (kept["gram"],)

    def order_first(after):
        kept["matrix"] = ordered(order, kept["split"], after, (0, tiles * 3 // 8))
        return (kept["matrix"],)

    def order_rest(after):
        kept["matrix"] = ordered(order, kept["split"], after, (tiles * 3 // 8, tiles), kept["matrix"])
        return (kept["matrix"],)

    def turn_work(after):
        kept["turned"], meets = turn(chosen, kept["matrix"], kept["turns"], after)
        kept["behind"] = from_behind(meets, "cols", -1)
        return (meets,)

    def moved_work(after):
        kept["moved"] = moved_block(order, came, kept["turns"], after)
        return (kept["moved"],)

    sums, last = couplings(chosen, held)
    came = from_behind(last, "cols", 1)
    sums, last_sums = summed(sums, "rows", [gram_work, order_first, order_rest])
    came_sums = from_behind(last_sums, "cols", 1)
    cross, own = cross_gram(chosen, kept["split"], came, sums)
    kept["turns"] = three_rotations(sums, came_sums, cross)

    sums = second_sums(chosen, kept["gram"], cross, own, kept["turns"])
    sums, last_sums = summed(sums, "rows", [turn_work, moved_work])
    behind_sums = from_behind(last_sums, "cols", -1)
    return finish(chosen, kept["turned"], kept["moved"], kept["behind"], three_rotations(sums, behind_sums))


def solution(mesh):
    placed = (P(("rows", "cols"), None, None), P("rows"), P())
    return jax.shard_map(
        body, mesh=mesh, in_specs=placed, out_specs=P("rows", "cols"), check_vma=False
    )
```

```python
import jax
import jax.numpy as jnp
from jax import lax
from jax.experimental import pallas as pl
from jax.experimental.pallas import tpu as pltpu
from jax.sharding import PartitionSpec as P

STEPS = 2
NS_STEPS = 6
SLOTS = 4
LANES = 128
WAYS = 2
PARTS = 4
MIB = 1024 * 1024

F32 = jnp.float32
BF16 = jnp.bfloat16
NN = (((1,), (0,)), ((), ()))
NT = (((1,), (1,)), ((), ()))
TN = (((0,), (0,)), ((), ()))

ANY = pl.BlockSpec(memory_space=pl.ANY)
HBM = pl.BlockSpec(memory_space=pltpu.HBM)
SMEM = pl.BlockSpec(memory_space=pltpu.SMEM)
VMEM = pl.BlockSpec(memory_space=pltpu.VMEM)


def pair_slots(chosen):
    partner = 2 - chosen
    low = jnp.where(partner == 0, 1, 0)
    high = jnp.where(partner == 2, 1, 2)
    return partner, low, high


def params(mib, flops=0, moved=0):
    return dict(
        compiler_params=pltpu.CompilerParams(vmem_limit_bytes=mib * MIB),
        cost_estimate=pl.CostEstimate(flops=int(flops), bytes_accessed=int(moved), transcendentals=0),
    )


def like(*arrays):
    return [jax.ShapeDtypeStruct(a.shape, a.dtype) for a in arrays]


def halves(value):
    high = value.astype(BF16)
    return high, (value - high.astype(F32)).astype(BF16)


def thirds(value):
    high = value.astype(BF16)
    rest = value - high.astype(F32)
    middle = rest.astype(BF16)
    return high, middle, (rest - middle.astype(F32)).astype(BF16)


def mul(a, b, dims=NN):
    return lax.dot_general(a, b, dims, preferred_element_type=F32)


def mul_split(a, b, dims=NN):
    return mul(a[0], b[0], dims) + (mul(a[0], b[1], dims) + mul(a[1], b[0], dims))


def dot_split(a, b, dims=NN):
    return mul_split(halves(a), halves(b), dims)


def identity(size):
    return lax.broadcasted_iota(jnp.int32, (size, size), 0) == lax.broadcasted_iota(jnp.int32, (size, size), 1)


def span(index, width):
    return pl.ds(pl.multiple_of(index * width, width), width)


def spread_kernel(tracks_ref, pieces_ref, came_ref, ready_ref, in_sems, out_sems):
    row_devices, frames, _, rows = came_ref.shape
    loads = [
        pltpu.make_async_copy(tracks_ref.at[:, :, pl.ds(r * rows, rows)], came_ref.at[r], in_sems.at[r])
        for r in range(row_devices)
    ]
    stores = [
        pltpu.make_async_copy(ready_ref.at[r], pieces_ref.at[r], out_sems.at[r]) for r in range(row_devices)
    ]
    for load in loads:
        load.start()
    for r in range(row_devices):
        loads[r].wait()
        for component in range(2):
            plane = came_ref[r, :, component, :]
            for group in range(frames // 8):
                for half in range(2):
                    ready_ref[r, 2 * component + half, 4 * group:4 * group + 4, :] = plane[
                        8 * group + 4 * half:8 * group + 4 * half + 4, :]
        stores[r].start()
    for store in stores:
        store.wait()


def spread(tracks, row_devices):
    frames, _, pixels = tracks.shape
    rows = pixels // row_devices
    shape = (row_devices, 4, frames // 2, rows)
    return pl.pallas_call(
        spread_kernel,
        in_specs=[ANY],
        out_specs=HBM,
        out_shape=jax.ShapeDtypeStruct(shape, F32),
        scratch_shapes=[
            pltpu.VMEM((row_devices, frames, 2, rows), F32),
            pltpu.VMEM(shape, F32),
            pltpu.SemaphoreType.DMA((row_devices,)),
            pltpu.SemaphoreType.DMA((row_devices,)),
        ],
        name="spread",
        **params(61, 0, 8 * tracks.size),
    )(tracks)


def loads_of(held_ref, came_ref, sems):
    loads = [
        pltpu.make_async_copy(held_ref.at[:, pl.ds(k * LANES, LANES)], came_ref.at[k], sems.at[k])
        for k in range(came_ref.shape[0])
    ]
    for load in loads:
        load.start()
    return loads


def loads_scratch(columns, rows):
    return [pltpu.VMEM((rows // LANES, columns, LANES), F32), pltpu.SemaphoreType.DMA((rows // LANES,))]


def coupling_kernel(chosen_ref, held_ref, sums_ref, last_ref, came_ref, sems):
    tiles = came_ref.shape[0]
    width = sums_ref.shape[1]
    loads = loads_of(held_ref, came_ref, sems)
    partner, first, second = pair_slots(chosen_ref[0])
    products = [jnp.zeros((2 * width, 2 * width), F32)] * 2
    squares = [jnp.zeros((width, LANES), F32)] * SLOTS
    for part in range(0, tiles, WAYS):
        here = range(part, part + WAYS)
        for k in here:
            loads[k].wait()
        for index, slots in enumerate(((partner, SLOTS - 1), (first, second))):
            both = []
            for side, slot in enumerate(slots):
                pieces = [came_ref[k, pl.ds(slot, width, SLOTS), :] for k in here]
                for piece in pieces:
                    squares[2 * index + side] += piece * piece
                block = jnp.concatenate(pieces, axis=1)
                if index == 0:
                    last_ref[side * width:(side + 1) * width, part * LANES:(part + WAYS) * LANES] = block
                both.append(jnp.concatenate(halves(block), axis=0))
            products[index] += mul(both[0], both[1], NT)
    for index, product in enumerate(products):
        top = product[:width, :width] + (product[:width, width:] + product[width:, :width])
        sums_ref[index * width:(index + 1) * width, :] = top + product[width:, width:]
    rows = [jnp.sum(squared.T, axis=0, keepdims=True) for squared in squares]
    sums_ref[2 * width:, :] = jnp.concatenate(rows + [jnp.zeros((4, width), F32)], axis=0)


def couplings(chosen, held):
    columns, rows = held.shape
    width = columns // SLOTS
    return pl.pallas_call(
        coupling_kernel,
        in_specs=[SMEM, ANY],
        out_specs=[VMEM] * 2,
        out_shape=[
            jax.ShapeDtypeStruct((2 * width + 8, width), F32),
            jax.ShapeDtypeStruct((2 * width, rows), F32),
        ],
        scratch_shapes=loads_scratch(columns, rows),
        name="couplings",
        **params(16, 16 * width * width * rows, 6 * held.size),
    )(chosen, held)


def gram_kernel(value_ref, held_ref, carried_ref, gram_ref, split_ref, came_ref, sems):
    tiles = came_ref.shape[0]
    columns = gram_ref.shape[0]
    width = columns // SLOTS
    loads = loads_of(held_ref, came_ref, sems)
    carried_ref[...] = value_ref[...]
    cross = 0.0
    for half in range(2):
        here = range(half * tiles // 2, (half + 1) * tiles // 2)
        for k in here:
            loads[k].wait()
            for slot in range(SLOTS):
                high, low = halves(came_ref[k, pl.ds(slot, width, SLOTS), :])
                lanes = slice(k * LANES, (k + 1) * LANES)
                split_ref[slot * width:(slot + 1) * width, lanes] = high
                split_ref[columns + slot * width:columns + (slot + 1) * width, lanes] = low
        lanes = slice(here.start * LANES, here.stop * LANES)
        high = split_ref[:columns, lanes]
        cross += mul(high, split_ref[columns:, lanes], NT)
        if half == 0:
            gram_ref[...] = mul(high, high, NT)
        else:
            gram_ref[...] += mul(high, high, NT) + (cross + cross.T)


def local_gram(value, held):
    columns, rows = held.shape
    return pl.pallas_call(
        gram_kernel,
        in_specs=[VMEM, ANY],
        out_specs=[VMEM] * 3,
        out_shape=like(value) + [
            jax.ShapeDtypeStruct((columns, columns), F32),
            jax.ShapeDtypeStruct((2 * columns, rows), BF16),
        ],
        scratch_shapes=loads_scratch(columns, rows),
        name="gram",
        **params(16, 4 * columns * columns * rows, 8 * columns * rows),
    )(value, held)


def left_terms(value):
    high, middle, low = thirds(value)
    return jnp.concatenate([high, middle], axis=1), jnp.concatenate([low, high], axis=1)


def right_terms(value):
    high, middle, low = thirds(value)
    wide = jnp.concatenate([high, middle], axis=1)
    return jnp.concatenate([wide, wide], axis=0), jnp.concatenate([high, low], axis=0)


def terms_product(left, right):
    width = left[0].shape[0]
    wide = mul(left[0], right[0])
    return wide[:, :width] + (wide[:, width:] + mul(left[1], right[1]))


def rotations(grams):
    width = grams[0][0].shape[0]
    eye = identity(width).astype(F32)
    couplings, scales, squares, products = [], [], [], []
    for block, row_sums, column_sums in grams:
        coupling = block / (jnp.broadcast_to(row_sums, (width, width)).T + column_sums)
        total = 1.0 + jnp.sum(coupling * coupling)
        couplings.append(coupling)
        flipped = coupling.T
        for one, two in ((coupling, flipped), (flipped, coupling)):
            scales.append(1.0 / jnp.sqrt(total))
            squares.append((eye + terms_product(left_terms(one), right_terms(two))) / total)
    for count in range(NS_STEPS):
        factors = [1.5 * eye - 0.5 * square for square in squares]
        rights = [right_terms(factor) for factor in factors]
        if count == 0:
            products = [scale * factor for scale, factor in zip(scales, factors)]
        else:
            products = [terms_product(left_terms(product), right) for product, right in zip(products, rights)]
        if count + 1 < NS_STEPS:
            for _ in range(2):
                squares = [terms_product(left_terms(square), right) for square, right in zip(squares, rights)]
    results = []
    for index, coupling in enumerate(couplings):
        across = terms_product(left_terms(products[2 * index]), right_terms(coupling))
        results.append((products[2 * index], across, -across.T, products[2 * index + 1]))
    return results


def rotation_kernel(one_ref, two_ref, rotation_ref, sent_ref):
    width = one_ref.shape[1]
    total = one_ref[...] + two_ref[...]
    sums = total[2 * width:]
    grams = [(total[:width], sums[0:1], sums[1:2]), (total[width:2 * width], sums[2:3], sums[3:4])]
    for index, (top, right, bottom, end) in enumerate(rotations(grams)):
        rotation_ref[index, :width, :width] = top
        rotation_ref[index, :width, width:] = right
        rotation_ref[index, width:, :width] = bottom
        rotation_ref[index, width:, width:] = end
        if index == 0:
            sent_ref[:width, :] = right
            sent_ref[width:, :] = end


def two_rotations(one, two):
    width = one.shape[1]
    return pl.pallas_call(
        rotation_kernel,
        in_specs=[VMEM] * 2,
        out_specs=[VMEM] * 2,
        out_shape=[
            jax.ShapeDtypeStruct((2, 2 * width, 2 * width), F32),
            jax.ShapeDtypeStruct((2 * width, width), F32),
        ],
        name="rotations",
        **params(16, 300 * 4 * width**3, 16 * width * width),
    )(one, two)


def own_kernel(chosen_ref, gram_ref, split_ref, came_ref, rotation_ref, sums_ref, meets_ref, pair_ref):
    width = sums_ref.shape[1]
    columns = SLOTS * width
    partner, first, second = pair_slots(chosen_ref[0])
    meets, low, high = pair_slots(chosen_ref[1])

    def place(slot):
        in_last = slot == partner
        members = (jnp.where(in_last, partner, first), jnp.where(in_last, SLOTS - 1, second))
        side = jnp.where(jnp.logical_or(in_last, slot == first), 0, 1)
        return members, rotation_ref[jnp.where(in_last, 0, 1), :, span(side, width)]

    def between(rows, others):
        return jnp.concatenate(
            [jnp.concatenate([gram_ref[span(r, width), span(c, width)] for c in others], axis=1) for r in rows], axis=0)

    def squares(gram, turn):
        return jnp.sum(turn * dot_split(gram, turn), axis=0, keepdims=True)

    (meets_in, meets_turn), (low_in, low_turn), (high_in, high_turn) = place(meets), place(low), place(high)
    here = [
        jnp.concatenate([split_ref[span(m + start, width), :] for m in meets_in], axis=0) for start in (0, SLOTS)
    ]
    came = halves(came_ref[...])
    meets_ref[...] = dot_split(meets_turn, mul_split(here, came, NT), TN)
    twice = mul(came[0], came[1], NT)
    pair_ref[...] = mul(came[0], came[0], NT) + (twice + twice.T)
    sums_ref[:width, :] = jnp.zeros((width, width), F32)
    sums_ref[width:2 * width, :] = dot_split(low_turn, dot_split(between(low_in, high_in), high_turn), TN)
    rows = [
        squares(between(meets_in, meets_in), meets_turn),
        jnp.zeros((1, width), F32),
        squares(between(low_in, low_in), low_turn),
        squares(between(high_in, high_in), high_turn),
        jnp.zeros((4, width), F32),
    ]
    sums_ref[2 * width:, :] = jnp.concatenate(rows, axis=0)


def own_sums(chosen, gram, split, came, turns):
    pair, rows = came.shape
    width = pair // 2
    return pl.pallas_call(
        own_kernel,
        in_specs=[SMEM] + [VMEM] * 4,
        out_specs=[VMEM] * 3,
        out_shape=[
            jax.ShapeDtypeStruct((2 * width + 8, width), F32),
            jax.ShapeDtypeStruct((width, pair), F32),
            jax.ShapeDtypeStruct((pair, pair), F32),
        ],
        name="own_sums",
        **params(16, 10 * pair * pair * rows, 8 * came.size),
    )(chosen, gram, split, came, turns)


def second_kernel(own_ref, meets_ref, pair_ref, turn_ref, sums_ref):
    width = sums_ref.shape[1]
    turn = turn_ref[...]
    split = halves(turn)
    sums_ref[...] = own_ref[...]
    sums_ref[:width, :] = mul_split(halves(meets_ref[...]), split)
    sums_ref[2 * width + 1:2 * width + 2, :] = jnp.sum(
        turn * mul_split(halves(pair_ref[...]), split), axis=0, keepdims=True)


def second_sums(own, meets, pair, came_turn):
    return pl.pallas_call(
        second_kernel,
        in_specs=[VMEM] * 4,
        out_specs=VMEM,
        out_shape=like(own)[0],
        name="second_sums",
        **params(8, 4 * pair.size * own.shape[1], 8 * pair.size),
    )(own, meets, pair, came_turn)


def picks(order_ref, rows):
    order = order_ref[...]
    return jnp.where(lax.broadcasted_iota(jnp.int32, (rows, order.shape[1]), 0) == order, 1.0, 0.0).astype(BF16)


def order_kernel(order_ref, split_ref, value_ref, *refs):
    carried_ref, matrix_ref = refs[-2:]
    width = matrix_ref.shape[3]

    @pl.when(pl.program_id(0) == 0)
    def _():
        carried_ref[...] = value_ref[...]

    both = mul(split_ref[...], picks(order_ref, split_ref.shape[1]))
    for term in range(2):
        for block in range(SLOTS):
            start = (term * SLOTS + block) * width
            matrix_ref[term, block] = both[start:start + width].T.astype(BF16)


def ordered(order, split, value, tiles, into=None):
    columns, rows = split.shape[0] // 2, split.shape[1]
    width = columns // SLOTS
    chunk = 2 * width
    start, stop = tiles
    extra = () if into is None else (into,)
    return pl.pallas_call(
        order_kernel,
        grid=(stop - start,),
        in_specs=[
            pl.BlockSpec((1, chunk), lambda k: (0, k + start)),
            VMEM,
            VMEM,
        ] + [ANY] * len(extra),
        out_specs=[VMEM, pl.BlockSpec((2, SLOTS, chunk, width), lambda k: (0, 0, k + start, 0))],
        out_shape=like(value) + [jax.ShapeDtypeStruct((2, SLOTS, rows, width), BF16)],
        input_output_aliases={} if into is None else {3: 1},
        name="row_order",
        **params(16, 4 * columns * rows * chunk * (stop - start), 8 * columns * rows),
    )(order, split, value, *extra)


def turn_kernel(chosen_ref, matrix_ref, rotation_ref, value_ref, carried_ref, turned_ref):
    width = matrix_ref.shape[3]
    partner, first, second = pair_slots(chosen_ref[0])

    @pl.when(pl.program_id(0) == 0)
    def _():
        carried_ref[...] = value_ref[...]

    for index, (one, two) in enumerate(((partner, SLOTS - 1), (first, second))):
        pair = [jnp.concatenate([matrix_ref[term, one], matrix_ref[term, two]], axis=1) for term in range(2)]
        turned = mul_split(pair, halves(rotation_ref[index]))
        for term, part in enumerate(halves(turned)):
            turned_ref[term, one] = part[:, :width]
            turned_ref[term, two] = part[:, width:]


def turn(chosen, matrix, turns, value):
    _, _, rows, width = matrix.shape
    chunk = rows // 2
    blocks = pl.BlockSpec((2, SLOTS, chunk, width), lambda k: (0, 0, k, 0))
    return pl.pallas_call(
        turn_kernel,
        grid=(rows // chunk,),
        in_specs=[SMEM, blocks, VMEM, VMEM],
        out_specs=[VMEM, blocks],
        out_shape=like(value, matrix),
        name="first_turn",
        **params(20, 24 * rows * width * width, 4 * matrix.size),
    )(chosen, matrix, turns, value)


def take_kernel(chosen_ref, turned_ref, value_ref, carried_ref, block_ref):
    slot = 2 - chosen_ref[1]
    carried_ref[...] = value_ref[...]
    block_ref[...] = turned_ref[0, slot].astype(F32) + turned_ref[1, slot].astype(F32)


def taken(chosen, turned, value):
    _, _, rows, width = turned.shape
    return pl.pallas_call(
        take_kernel,
        in_specs=[SMEM, VMEM, VMEM],
        out_specs=[VMEM, VMEM],
        out_shape=like(value) + [jax.ShapeDtypeStruct((rows, width), F32)],
        name="taken",
        **params(8, 0, 8 * rows * width),
    )(chosen, turned, value)


def moved_kernel(order_ref, came_ref, turn_ref, value_ref, carried_ref, block_ref, split_ref):
    width = block_ref.shape[2]
    rows = came_ref.shape[1]

    @pl.when(pl.program_id(0) == 0)
    def _():
        carried_ref[...] = value_ref[...]
        high, low = halves(dot_split(turn_ref[...], came_ref[...], TN))
        split_ref[:width, :] = high
        split_ref[width:, :] = low

    both = mul(split_ref[...], picks(order_ref, rows))
    for term in range(2):
        block_ref[term] = both[term * width:(term + 1) * width].T.astype(BF16)


def moved_block(order, came, came_turn, value):
    pair, rows = came.shape
    width = pair // 2
    chunk = pair
    return pl.pallas_call(
        moved_kernel,
        grid=(rows // chunk,),
        in_specs=[
            pl.BlockSpec((1, chunk), lambda k: (0, k)),
            VMEM,
            VMEM,
            VMEM,
        ],
        out_specs=[VMEM, pl.BlockSpec((2, chunk, width), lambda k: (0, k, 0))],
        out_shape=like(value) + [jax.ShapeDtypeStruct((2, rows, width), BF16)],
        scratch_shapes=[pltpu.VMEM((pair, rows), BF16)],
        name="moved_block",
        **params(16, 4 * width * rows * rows, 8 * came.size),
    )(order, came, came_turn, value)


def most_kernel(chosen_ref, turned_ref, moved_ref, rotation_ref, out_ref, ready_ref, sems):
    rows, width = moved_ref.shape[1:]
    meets, low, high = pair_slots(chosen_ref[1])
    chunk = rows // PARTS
    pair_turn = halves(rotation_ref[1])
    meets_turn = halves(rotation_ref[0, :, :width])
    stores = []
    for part in range(PARTS):
        here = pl.ds(part * chunk, chunk)

        def beside(one, two):
            return [jnp.concatenate([one[term], two[term]], axis=1) for term in range(2)]

        def block(slot, here=here):
            return [turned_ref[term, slot, here] for term in range(2)]

        pair = mul_split(beside(block(low), block(high)), pair_turn)
        ready_ref[here, span(low, width)] = pair[:, :width]
        ready_ref[here, span(high, width)] = pair[:, width:]
        ready_ref[here, span(meets, width)] = mul_split(
            beside(block(meets), [moved_ref[term, here] for term in range(2)]), meets_turn)
        stores.append(pltpu.make_async_copy(
            ready_ref.at[here], out_ref.at[here, pl.ds(0, (SLOTS - 1) * width)], sems.at[part]))
        stores[-1].start()
    for store in stores:
        store.wait()


def most_slots(chosen, turned, moved, turns):
    _, _, rows, width = turned.shape
    return pl.pallas_call(
        most_kernel,
        in_specs=[SMEM] + [VMEM] * 3,
        out_specs=ANY,
        out_shape=jax.ShapeDtypeStruct((rows, SLOTS * width), F32),
        scratch_shapes=[pltpu.VMEM((rows, (SLOTS - 1) * width), F32), pltpu.SemaphoreType.DMA((PARTS,))],
        name="second_turn",
        **params(16, 18 * rows * width * width, 4 * turned.size),
    )(chosen, turned, moved, turns)


def rest_kernel(turned_ref, behind_ref, turn_ref, _, out_ref, ready_ref, sems):
    rows, width = behind_ref.shape
    chunk = rows // PARTS
    split = halves(turn_ref[...])
    stores = []
    for part in range(PARTS):
        here = pl.ds(part * chunk, chunk)
        pair = [
            jnp.concatenate([one, turned_ref[term, SLOTS - 1, here]], axis=1)
            for term, one in enumerate(halves(behind_ref[here]))
        ]
        ready_ref[here] = mul_split(pair, split)
        stores.append(pltpu.make_async_copy(
            ready_ref.at[here], out_ref.at[here, pl.ds((SLOTS - 1) * width, width)], sems.at[part]))
        stores[-1].start()
    for store in stores:
        store.wait()


def last_slot(turned, behind, behind_turn, out):
    _, _, rows, width = turned.shape
    return pl.pallas_call(
        rest_kernel,
        in_specs=[VMEM] * 3 + [ANY],
        out_specs=ANY,
        out_shape=like(out)[0],
        scratch_shapes=[pltpu.VMEM((rows, width), F32), pltpu.SemaphoreType.DMA((PARTS,))],
        input_output_aliases={3: 0},
        name="last_slot",
        **params(16, 12 * rows * width * width, 12 * rows * width),
    )(turned, behind, behind_turn, out)


def from_behind(value, axis, steps):
    count = lax.axis_size(axis)
    pairs = [(source, (source + steps) % count) for source in range(count)]
    return lax.ppermute(value, axis, pairs)


def summed(value, axis, beside):
    count = lax.axis_size(axis)
    got = jnp.zeros_like(value)
    if count & (count - 1):
        value, count = lax.psum(value, axis), 1
    distance = 1
    while distance < count:
        if distance > 1:
            value = value + got
        got = lax.ppermute(value, axis, [(source, source ^ distance) for source in range(count)])
        if beside:
            value = beside.pop(0)(value)
        distance *= 2
    for work in beside:
        value = work(value)
    return value, got


def body(tracks, pixel_order, pairing):
    frames_dev, _, pixel_total = tracks.shape
    row_devices = lax.axis_size("rows")
    row_count = pixel_total // row_devices
    pieces = spread(tracks, row_devices).reshape(row_devices * 4, frames_dev // 2, row_count)
    arrived = lax.all_to_all(pieces, ("rows", "cols"), split_axis=0, concat_axis=0, tiled=True)
    held = arrived.reshape(-1, row_count)
    order = (pixel_order - lax.axis_index("rows") * row_count).reshape(1, row_count)
    chosen = lax.dynamic_index_in_dim(pairing, lax.axis_index("cols"), axis=1, keepdims=False)
    tiles = row_count // (held.shape[0] // 2)
    kept = {}

    def gram_work(value):
        value, kept["gram"], kept["split"] = local_gram(value, held)
        return value

    def order_first(value):
        value, kept["matrix"] = ordered(order, kept["split"], value, (0, tiles // 2))
        return value

    def order_rest(value):
        value, kept["matrix"] = ordered(order, kept["split"], value, (tiles // 2, tiles), kept["matrix"])
        return value

    def turn_work(value):
        value, kept["turned"] = turn(chosen, kept["matrix"], turns, value)
        return value

    def taken_work(value):
        value, meets = taken(chosen, kept["turned"], value)
        kept["behind"] = from_behind(meets, "cols", -1)
        return value

    def moved_work(value):
        value, kept["moved"] = moved_block(order, came, came_turn, value)
        return value

    sums, last = couplings(chosen, held)
    came = from_behind(last, "cols", 1)
    turns, sent = two_rotations(*summed(sums, "rows", [gram_work, order_first, order_rest]))
    came_turn = from_behind(sent, "cols", 1)
    own, meets, pair = own_sums(chosen, kept["gram"], kept["split"], came, turns)
    sums = second_sums(own, meets, pair, came_turn)

    second_turns, sent = two_rotations(*summed(sums, "rows", [turn_work, taken_work, moved_work]))
    behind_turn = from_behind(sent, "cols", -1)
    out = most_slots(chosen, kept["turned"], kept["moved"], second_turns)
    return last_slot(kept["turned"], kept["behind"], behind_turn, out)


def solution(mesh):
    placed = (P(("rows", "cols"), None, None), P("rows"), P())
    return jax.shard_map(
        body, mesh=mesh, in_specs=placed, out_specs=P("rows", "cols"), check_vma=False
    )
```

```python
import jax
import jax.numpy as jnp
from jax import lax
from jax.experimental import pallas as pl
from jax.experimental.pallas import tpu as pltpu
from jax.sharding import PartitionSpec as P

STEPS = 2
NS_STEPS = 6
SLOTS = 4
LANES = 128
WAYS = 2
PARTS = 8
MIB = 1024 * 1024

F32 = jnp.float32
BF16 = jnp.bfloat16
NN = (((1,), (0,)), ((), ()))
NT = (((1,), (1,)), ((), ()))
TN = (((0,), (0,)), ((), ()))

ANY = pl.BlockSpec(memory_space=pl.ANY)
HBM = pl.BlockSpec(memory_space=pltpu.HBM)
SMEM = pl.BlockSpec(memory_space=pltpu.SMEM)
VMEM = pl.BlockSpec(memory_space=pltpu.VMEM)


def pair_slots(chosen):
    partner = 2 - chosen
    low = jnp.where(partner == 0, 1, 0)
    high = jnp.where(partner == 2, 1, 2)
    return partner, low, high


def params(mib, flops=0, moved=0):
    return dict(
        compiler_params=pltpu.CompilerParams(vmem_limit_bytes=mib * MIB),
        cost_estimate=pl.CostEstimate(flops=int(flops), bytes_accessed=int(moved), transcendentals=0),
    )


def like(*arrays):
    return [jax.ShapeDtypeStruct(a.shape, a.dtype) for a in arrays]


def halves(value):
    high = value.astype(BF16)
    return high, (value - high.astype(F32)).astype(BF16)


def thirds(value):
    high = value.astype(BF16)
    rest = value - high.astype(F32)
    middle = rest.astype(BF16)
    return high, middle, (rest - middle.astype(F32)).astype(BF16)


def mul(a, b, dims=NN):
    return lax.dot_general(a, b, dims, preferred_element_type=F32)


def mul_split(a, b, dims=NN):
    return mul(a[0], b[0], dims) + (mul(a[0], b[1], dims) + mul(a[1], b[0], dims))


def dot_split(a, b, dims=NN):
    return mul_split(halves(a), halves(b), dims)


def identity(size):
    return lax.broadcasted_iota(jnp.int32, (size, size), 0) == lax.broadcasted_iota(jnp.int32, (size, size), 1)


def span(index, width):
    return pl.ds(pl.multiple_of(index * width, width), width)


def spread_kernel(tracks_ref, pieces_ref, came_ref, ready_ref, in_sems, out_sems):
    row_devices, frames, _, rows = came_ref.shape
    loads = [
        pltpu.make_async_copy(tracks_ref.at[:, :, pl.ds(r * rows, rows)], came_ref.at[r], in_sems.at[r])
        for r in range(row_devices)
    ]
    stores = [
        pltpu.make_async_copy(ready_ref.at[r], pieces_ref.at[r], out_sems.at[r]) for r in range(row_devices)
    ]
    for load in loads:
        load.start()
    for r in range(row_devices):
        loads[r].wait()
        for component in range(2):
            plane = came_ref[r, :, component, :]
            for group in range(frames // 8):
                for half in range(2):
                    ready_ref[r, 2 * component + half, 4 * group:4 * group + 4, :] = plane[
                        8 * group + 4 * half:8 * group + 4 * half + 4, :]
        stores[r].start()
    for store in stores:
        store.wait()


def spread(tracks, row_devices):
    frames, _, pixels = tracks.shape
    rows = pixels // row_devices
    shape = (row_devices, 4, frames // 2, rows)
    return pl.pallas_call(
        spread_kernel,
        in_specs=[ANY],
        out_specs=HBM,
        out_shape=jax.ShapeDtypeStruct(shape, F32),
        scratch_shapes=[
            pltpu.VMEM((row_devices, frames, 2, rows), F32),
            pltpu.VMEM(shape, F32),
            pltpu.SemaphoreType.DMA((row_devices,)),
            pltpu.SemaphoreType.DMA((row_devices,)),
        ],
        name="spread",
        **params(61, 0, 8 * tracks.size),
    )(tracks)


def coupling_kernel(chosen_ref, held_ref, sums_ref, one_ref, two_ref, came_ref, sems):
    tiles = came_ref.shape[0]
    width = sums_ref.shape[1]
    loads = [
        pltpu.make_async_copy(held_ref.at[:, pl.ds(k * LANES, LANES)], came_ref.at[k], sems.at[k])
        for k in range(tiles)
    ]
    for load in loads:
        load.start()
    partner, first, second = pair_slots(chosen_ref[0])
    products = [jnp.zeros((2 * width, 2 * width), F32)] * 2
    squares = [jnp.zeros((width, LANES), F32)] * SLOTS
    for part in range(0, tiles, WAYS):
        here = range(part, part + WAYS)
        for k in here:
            loads[k].wait()
        for index, slots in enumerate(((partner, SLOTS - 1), (first, second))):
            both = []
            for side, slot in enumerate(slots):
                pieces = [came_ref[k, pl.ds(slot, width, SLOTS), :] for k in here]
                for piece in pieces:
                    squares[2 * index + side] += piece * piece
                block = jnp.concatenate(pieces, axis=1)
                if index == 0:
                    (one_ref, two_ref)[side][:, part * LANES:(part + WAYS) * LANES] = block
                both.append(jnp.concatenate(halves(block), axis=0))
            products[index] += mul(both[0], both[1], NT)
    for index, product in enumerate(products):
        top = product[:width, :width] + (product[:width, width:] + product[width:, :width])
        sums_ref[index * width:(index + 1) * width, :] = top + product[width:, width:]
    rows = [jnp.sum(squared.T, axis=0, keepdims=True) for squared in squares]
    sums_ref[2 * width:, :] = jnp.concatenate(rows + [jnp.zeros((4, width), F32)], axis=0)


def couplings(chosen, held):
    columns, rows = held.shape
    width = columns // SLOTS
    return pl.pallas_call(
        coupling_kernel,
        in_specs=[SMEM, ANY],
        out_specs=[VMEM] * 4,
        out_shape=[
            jax.ShapeDtypeStruct((2 * width + 8, width), F32),
            jax.ShapeDtypeStruct((width, rows), F32),
            jax.ShapeDtypeStruct((width, rows), F32),
            jax.ShapeDtypeStruct((rows // LANES, columns, LANES), F32),
        ],
        scratch_shapes=[pltpu.SemaphoreType.DMA((rows // LANES,))],
        name="couplings",
        **params(16, 16 * width * width * rows, 6 * held.size),
    )(chosen, held)


def gram_kernel(value_ref, came_ref, carried_ref, gram_ref, split_ref):
    tiles = came_ref.shape[0]
    columns = gram_ref.shape[0]
    width = columns // SLOTS
    carried_ref[...] = value_ref[...]
    cross = 0.0
    for half in range(2):
        here = range(half * tiles // 2, (half + 1) * tiles // 2)
        for k in here:
            for slot in range(SLOTS):
                high, low = halves(came_ref[k, pl.ds(slot, width, SLOTS), :])
                lanes = slice(k * LANES, (k + 1) * LANES)
                split_ref[slot * width:(slot + 1) * width, lanes] = high
                split_ref[columns + slot * width:columns + (slot + 1) * width, lanes] = low
        lanes = slice(here.start * LANES, here.stop * LANES)
        high = split_ref[:columns, lanes]
        cross += mul(high, split_ref[columns:, lanes], NT)
        if half == 0:
            gram_ref[...] = mul(high, high, NT)
        else:
            gram_ref[...] += mul(high, high, NT) + (cross + cross.T)


def local_gram(value, came):
    tiles, columns, lanes = came.shape
    rows = tiles * lanes
    return pl.pallas_call(
        gram_kernel,
        in_specs=[VMEM] * 2,
        out_specs=[VMEM] * 3,
        out_shape=like(value) + [
            jax.ShapeDtypeStruct((columns, columns), F32),
            jax.ShapeDtypeStruct((2 * columns, rows), BF16),
        ],
        name="gram",
        **params(16, 4 * columns * columns * rows, 8 * columns * rows),
    )(value, came)


def left_terms(value):
    high, middle, low = thirds(value)
    return jnp.concatenate([high, middle], axis=1), jnp.concatenate([low, high], axis=1)


def right_terms(value):
    high, middle, low = thirds(value)
    wide = jnp.concatenate([high, middle], axis=1)
    return jnp.concatenate([wide, wide], axis=0), jnp.concatenate([high, low], axis=0)


def terms_product(left, right):
    width = right[1].shape[1]
    wide = mul(left[0], right[0])
    return wide[:, :width] + (wide[:, width:] + mul(left[1], right[1]))


def rotations(grams):
    width = grams[0][0].shape[0]
    eye = identity(width).astype(F32)
    couplings, scales, squares, products, crossed = [], [], [], [], []
    for block, row_sums, column_sums in grams:
        coupling = block / (jnp.broadcast_to(row_sums, (width, width)).T + column_sums)
        total = 1.0 + jnp.sum(coupling * coupling)
        couplings.append(coupling)
        flipped = coupling.T
        for one, two in ((coupling, flipped), (flipped, coupling)):
            scales.append(1.0 / jnp.sqrt(total))
            squares.append((eye + terms_product(left_terms(one), right_terms(two))) * (1.0 / total))
    for count in range(NS_STEPS):
        factors = [1.5 * eye - 0.5 * square for square in squares]
        rights = [right_terms(factor) for factor in factors]
        if count + 1 == NS_STEPS:
            crossed = [
                terms_product(left_terms(product), right_terms(coupling))
                for product, coupling in zip(products[::2], couplings)
            ]
        last = count + 1 == NS_STEPS
        if count == 0:
            products = [scale * factor for scale, factor in zip(scales, factors)]
        elif last:
            products = [terms_product(left_terms(product), right) for product, right in zip(products, rights)]
        else:
            both = [jnp.concatenate([square, product], axis=0) for square, product in zip(squares, products)]
            both = [terms_product(left_terms(one), right) for one, right in zip(both, rights)]
            squares, products = [one[:width] for one in both], [one[width:] for one in both]
        if count == 0:
            squares = [terms_product(left_terms(square), right) for square, right in zip(squares, rights)]
        if not last:
            squares = [terms_product(left_terms(square), right) for square, right in zip(squares, rights)]
    results = []
    for index, half in enumerate(crossed):
        across = terms_product(left_terms(factors[2 * index]), right_terms(half))
        results.append((products[2 * index], across, -across.T, products[2 * index + 1]))
    return results


def rotation_kernel(one_ref, two_ref, rotation_ref, sent_ref):
    width = one_ref.shape[1]
    total = one_ref[...] + two_ref[...]
    sums = total[2 * width:]
    grams = [(total[:width], sums[0:1], sums[1:2]), (total[width:2 * width], sums[2:3], sums[3:4])]
    for index, (top, right, bottom, end) in enumerate(rotations(grams)):
        rotation_ref[index, :width, :width] = top
        rotation_ref[index, :width, width:] = right
        rotation_ref[index, width:, :width] = bottom
        rotation_ref[index, width:, width:] = end
        if index == 0:
            sent_ref[:width, :] = right
            sent_ref[width:, :] = end


def two_rotations(one, two):
    width = one.shape[1]
    return pl.pallas_call(
        rotation_kernel,
        in_specs=[VMEM] * 2,
        out_specs=[VMEM] * 2,
        out_shape=[
            jax.ShapeDtypeStruct((2, 2 * width, 2 * width), F32),
            jax.ShapeDtypeStruct((2 * width, width), F32),
        ],
        name="rotations",
        **params(16, 300 * 4 * width**3, 16 * width * width),
    )(one, two)


def near(split_ref, slots, width):
    return [
        jnp.concatenate([split_ref[span(slot + start, width), :] for slot in slots], axis=0) for start in (0, SLOTS)
    ]


def places(chosen_ref):
    partner, first, second = pair_slots(chosen_ref[0])

    def place(slot):
        in_last = slot == partner
        members = (jnp.where(in_last, partner, first), jnp.where(in_last, SLOTS - 1, second))
        return members, jnp.where(in_last, 0, 1), jnp.where(jnp.logical_or(in_last, slot == first), 0, 1)

    return [place(slot) for slot in pair_slots(chosen_ref[1])]


def own_kernel(chosen_ref, gram_ref, split_ref, came_ref, rotation_ref, sums_ref, cross_ref, pair_ref):
    width = sums_ref.shape[1]

    def between(rows, others):
        return jnp.concatenate(
            [jnp.concatenate([gram_ref[span(r, width), span(c, width)] for c in others], axis=1) for r in rows], axis=0)

    def squares(gram, turn):
        return jnp.sum(turn * dot_split(gram, turn), axis=0, keepdims=True)

    found = places(chosen_ref)
    (meets_in, low_in, high_in), (meets_turn, low_turn, high_turn) = [members for members, _, _ in found], [
        rotation_ref[pair, :, span(side, width)] for _, pair, side in found
    ]
    here = near(split_ref, meets_in, width)
    came = halves(came_ref[...])
    pair = 2 * width
    by_high = mul(jnp.concatenate([*here, came[0]], axis=0), came[0], NT)
    by_low = mul(jnp.concatenate([here[0], came[0]], axis=0), came[1], NT)
    cross_ref[...] = by_high[:pair] + (by_high[pair:2 * pair] + by_low[:pair])
    pair_ref[...] = by_high[2 * pair:] + (by_low[pair:] + by_low[pair:].T)
    sums_ref[:width, :] = jnp.zeros((width, width), F32)
    sums_ref[width:2 * width, :] = dot_split(low_turn, dot_split(between(low_in, high_in), high_turn), TN)
    rows = [
        squares(between(meets_in, meets_in), meets_turn),
        jnp.zeros((1, width), F32),
        squares(between(low_in, low_in), low_turn),
        squares(between(high_in, high_in), high_turn),
        jnp.zeros((4, width), F32),
    ]
    sums_ref[2 * width:, :] = jnp.concatenate(rows, axis=0)


def own_sums(chosen, gram, split, came, turns):
    width, rows = came.shape
    return pl.pallas_call(
        own_kernel,
        in_specs=[SMEM] + [VMEM] * 4,
        out_specs=[VMEM] * 3,
        out_shape=[
            jax.ShapeDtypeStruct((2 * width + 8, width), F32),
            jax.ShapeDtypeStruct((2 * width, width), F32),
            jax.ShapeDtypeStruct((width, width), F32),
        ],
        name="own_sums",
        **params(16, 16 * width * width * rows, 24 * width * rows),
    )(chosen, gram, split, came, turns)


def cross_kernel(chosen_ref, split_ref, first_ref, second_ref, cross_ref, top_ref, rotation_ref, meets_ref, pair_ref):
    width = first_ref.shape[0]
    members, index, side = places(chosen_ref)[0]
    turn = rotation_ref[index, :, span(side, width)]
    here = near(split_ref, members, width)
    first, second = halves(first_ref[...]), halves(second_ref[...])
    pair = 2 * width
    by_high = mul(jnp.concatenate([*here, *first, second[0]], axis=0), second[0], NT)
    by_low = mul(jnp.concatenate([here[0], first[0], second[0]], axis=0), second[1], NT)
    cross = by_high[:pair] + (by_high[pair:2 * pair] + by_low[:pair])
    meets_ref[...] = dot_split(turn, jnp.concatenate([cross_ref[...], cross], axis=1), TN)
    rest = by_high[2 * pair:]
    mixed = rest[:width] + (rest[width:pair] + by_low[pair:pair + width])
    twice = by_low[pair + width:]
    pair_ref[:width, :width] = top_ref[...]
    pair_ref[:width, width:] = mixed
    pair_ref[width:, :width] = mixed.T
    pair_ref[width:, width:] = rest[pair:] + (twice + twice.T)


def came_sums(chosen, split, came, cross, top, turns):
    width, rows = came[0].shape
    return pl.pallas_call(
        cross_kernel,
        in_specs=[SMEM] + [VMEM] * 6,
        out_specs=[VMEM] * 2,
        out_shape=[
            jax.ShapeDtypeStruct((width, 2 * width), F32),
            jax.ShapeDtypeStruct((2 * width, 2 * width), F32),
        ],
        name="came_sums",
        **params(16, 16 * width * width * rows, 28 * width * rows),
    )(chosen, split, *came, cross, top, turns)


def second_kernel(own_ref, meets_ref, pair_ref, turn_ref, sums_ref):
    width = sums_ref.shape[1]
    turn = turn_ref[...]
    split = halves(turn)
    sums_ref[...] = own_ref[...]
    sums_ref[:width, :] = mul_split(halves(meets_ref[...]), split)
    sums_ref[2 * width + 1:2 * width + 2, :] = jnp.sum(
        turn * mul_split(halves(pair_ref[...]), split), axis=0, keepdims=True)


def second_sums(own, meets, pair, came_turn):
    return pl.pallas_call(
        second_kernel,
        in_specs=[VMEM] * 4,
        out_specs=VMEM,
        out_shape=like(own)[0],
        name="second_sums",
        **params(8, 4 * pair.size * own.shape[1], 8 * pair.size),
    )(own, meets, pair, came_turn)


def picks(order_ref, rows):
    order = order_ref[...]
    return jnp.where(lax.broadcasted_iota(jnp.int32, (rows, order.shape[1]), 0) == order, 1.0, 0.0).astype(BF16)


def order_kernel(order_ref, split_ref, value_ref, *refs):
    carried_ref, matrix_ref = refs[-2:]
    width = matrix_ref.shape[3]

    @pl.when(pl.program_id(0) == 0)
    def _():
        carried_ref[...] = value_ref[...]

    both = mul(split_ref[...], picks(order_ref, split_ref.shape[1]))
    for term in range(2):
        for block in range(SLOTS):
            start = (term * SLOTS + block) * width
            matrix_ref[term, block] = both[start:start + width].T.astype(BF16)


def ordered(order, split, value, tiles, into=None):
    columns, rows = split.shape[0] // 2, split.shape[1]
    width = columns // SLOTS
    chunk = 2 * width
    start, stop = tiles
    extra = () if into is None else (into,)
    return pl.pallas_call(
        order_kernel,
        grid=(stop - start,),
        in_specs=[
            pl.BlockSpec((1, chunk), lambda k: (0, k + start)),
            VMEM,
            VMEM,
        ] + [ANY] * len(extra),
        out_specs=[VMEM, pl.BlockSpec((2, SLOTS, chunk, width), lambda k: (0, 0, k + start, 0))],
        out_shape=like(value) + [jax.ShapeDtypeStruct((2, SLOTS, rows, width), BF16)],
        input_output_aliases={} if into is None else {3: 1},
        name="row_order",
        **params(16, 4 * columns * rows * chunk * (stop - start), 8 * columns * rows),
    )(order, split, value, *extra)


def turn_kernel(chosen_ref, matrix_ref, rotation_ref, value_ref, carried_ref, turned_ref, meets_ref):
    width = matrix_ref.shape[3]
    partner, first, second = pair_slots(chosen_ref[0])

    @pl.when(pl.program_id(0) == 0)
    def _():
        carried_ref[...] = value_ref[...]

    for index, (one, two) in enumerate(((partner, SLOTS - 1), (first, second))):
        pair = [jnp.concatenate([matrix_ref[term, one], matrix_ref[term, two]], axis=1) for term in range(2)]
        turned = mul_split(pair, halves(rotation_ref[index]))
        for term, part in enumerate(halves(turned)):
            turned_ref[term, one] = part[:, :width]
            turned_ref[term, two] = part[:, width:]
    slot = 2 - chosen_ref[1]
    meets_ref[...] = turned_ref[0, slot].astype(F32) + turned_ref[1, slot].astype(F32)


def turn(chosen, matrix, turns, value):
    _, _, rows, width = matrix.shape
    chunk = rows // 2
    blocks = pl.BlockSpec((2, SLOTS, chunk, width), lambda k: (0, 0, k, 0))
    return pl.pallas_call(
        turn_kernel,
        grid=(rows // chunk,),
        in_specs=[SMEM, blocks, VMEM, VMEM],
        out_specs=[VMEM, blocks, pl.BlockSpec((chunk, width), lambda k: (k, 0))],
        out_shape=like(value, matrix) + [jax.ShapeDtypeStruct((rows, width), F32)],
        name="first_turn",
        **params(20, 24 * rows * width * width, 4 * matrix.size),
    )(chosen, matrix, turns, value)


def moved_kernel(order_ref, one_ref, two_ref, turn_ref, value_ref, carried_ref, block_ref, split_ref):
    width = block_ref.shape[2]
    rows = one_ref.shape[1]

    @pl.when(pl.program_id(0) == 0)
    def _():
        carried_ref[...] = value_ref[...]
        high, low = halves(
            dot_split(turn_ref[...], jnp.concatenate([one_ref[...], two_ref[...]], axis=0), TN))
        split_ref[:width, :] = high
        split_ref[width:, :] = low

    both = mul(split_ref[...], picks(order_ref, rows))
    for term in range(2):
        block_ref[term] = both[term * width:(term + 1) * width].T.astype(BF16)


def moved_block(order, came, came_turn, value):
    width, rows = came[0].shape
    pair = chunk = 2 * width
    return pl.pallas_call(
        moved_kernel,
        grid=(rows // chunk,),
        in_specs=[
            pl.BlockSpec((1, chunk), lambda k: (0, k)),
            VMEM,
            VMEM,
            VMEM,
            VMEM,
        ],
        out_specs=[VMEM, pl.BlockSpec((2, chunk, width), lambda k: (0, k, 0))],
        out_shape=like(value) + [jax.ShapeDtypeStruct((2, rows, width), BF16)],
        scratch_shapes=[pltpu.VMEM((pair, rows), BF16)],
        name="moved_block",
        **params(16, 4 * width * rows * rows, 8 * pair * rows),
    )(order, *came, came_turn, value)


def most_kernel(chosen_ref, turned_ref, moved_ref, rotation_ref, out_ref, ready_ref, sems):
    rows, width = moved_ref.shape[1:]
    meets, low, high = pair_slots(chosen_ref[1])
    chunk = rows // PARTS
    pair_turn = halves(rotation_ref[1])
    meets_turn = halves(rotation_ref[0, :, :width])
    stores = []
    for part in range(PARTS):
        here = pl.ds(part * chunk, chunk)

        def beside(one, two):
            return [jnp.concatenate([one[term], two[term]], axis=1) for term in range(2)]

        def block(slot, here=here):
            return [turned_ref[term, slot, here] for term in range(2)]

        pair = mul_split(beside(block(low), block(high)), pair_turn)
        ready_ref[here, span(low, width)] = pair[:, :width]
        ready_ref[here, span(high, width)] = pair[:, width:]
        ready_ref[here, span(meets, width)] = mul_split(
            beside(block(meets), [moved_ref[term, here] for term in range(2)]), meets_turn)
        stores.append(pltpu.make_async_copy(
            ready_ref.at[here], out_ref.at[here, pl.ds(0, (SLOTS - 1) * width)], sems.at[part]))
        stores[-1].start()
    for store in stores:
        store.wait()


def most_slots(chosen, turned, moved, turns):
    _, _, rows, width = turned.shape
    return pl.pallas_call(
        most_kernel,
        in_specs=[SMEM] + [VMEM] * 3,
        out_specs=ANY,
        out_shape=jax.ShapeDtypeStruct((rows, SLOTS * width), F32),
        scratch_shapes=[pltpu.VMEM((rows, (SLOTS - 1) * width), F32), pltpu.SemaphoreType.DMA((PARTS,))],
        name="second_turn",
        **params(16, 18 * rows * width * width, 4 * turned.size),
    )(chosen, turned, moved, turns)


def rest_kernel(turned_ref, behind_ref, turn_ref, _, out_ref, ready_ref, sems):
    rows, width = behind_ref.shape
    chunk = rows // PARTS
    split = halves(turn_ref[...])
    stores = []
    for part in range(PARTS):
        here = pl.ds(part * chunk, chunk)
        pair = [
            jnp.concatenate([one, turned_ref[term, SLOTS - 1, here]], axis=1)
            for term, one in enumerate(halves(behind_ref[here]))
        ]
        ready_ref[here] = mul_split(pair, split)
        stores.append(pltpu.make_async_copy(
            ready_ref.at[here], out_ref.at[here, pl.ds((SLOTS - 1) * width, width)], sems.at[part]))
        stores[-1].start()
    for store in stores:
        store.wait()


def last_slot(turned, behind, behind_turn, out):
    _, _, rows, width = turned.shape
    return pl.pallas_call(
        rest_kernel,
        in_specs=[VMEM] * 3 + [ANY],
        out_specs=ANY,
        out_shape=like(out)[0],
        scratch_shapes=[pltpu.VMEM((rows, width), F32), pltpu.SemaphoreType.DMA((PARTS,))],
        input_output_aliases={3: 0},
        name="last_slot",
        **params(16, 12 * rows * width * width, 12 * rows * width),
    )(turned, behind, behind_turn, out)


def from_behind(value, axis, steps):
    count = lax.axis_size(axis)
    pairs = [(source, (source + steps) % count) for source in range(count)]
    return lax.ppermute(value, axis, pairs)


def summed(value, axis, beside):
    count = lax.axis_size(axis)
    got = jnp.zeros_like(value)
    if count & (count - 1):
        value, count = lax.psum(value, axis), 1
    distance = 1
    while distance < count:
        if distance > 1:
            value = value + got
        got = lax.ppermute(value, axis, [(source, source ^ distance) for source in range(count)])
        if beside:
            value = beside.pop(0)(value)
        distance *= 2
    for work in beside:
        value = work(value)
    return value, got


def body(tracks, pixel_order, pairing):
    frames_dev, _, pixel_total = tracks.shape
    row_devices = lax.axis_size("rows")
    row_count = pixel_total // row_devices
    pieces = spread(tracks, row_devices).reshape(row_devices * 4, frames_dev // 2, row_count)
    arrived = lax.all_to_all(pieces, ("rows", "cols"), split_axis=0, concat_axis=0, tiled=True)
    held = arrived.reshape(-1, row_count)
    order = (pixel_order - lax.axis_index("rows") * row_count).reshape(1, row_count)
    chosen = lax.dynamic_index_in_dim(pairing, lax.axis_index("cols"), axis=1, keepdims=False)
    chunks = row_count // (held.shape[0] // 2)
    kept = {}

    def gram_work(value):
        value, kept["gram"], kept["split"] = local_gram(value, tiles)
        return value

    def order_first(value):
        value, kept["matrix"] = ordered(order, kept["split"], value, (0, chunks * 3 // 8))
        return value

    def order_rest(value):
        value, kept["matrix"] = ordered(order, kept["split"], value, (chunks * 3 // 8, chunks), kept["matrix"])
        return value

    def turn_work(value):
        value, kept["turned"], kept["meets"] = turn(chosen, kept["matrix"], turns, value)
        return value

    def taken_work(value):
        value, meets = lax.optimization_barrier((value, kept["meets"]))
        kept["behind"] = from_behind(meets, "cols", -1)
        return value

    def moved_work(value):
        value, kept["moved"] = moved_block(order, came, came_turn, value)
        return value

    sums, *last, tiles = couplings(chosen, held)
    came = [from_behind(block, "cols", 1) for block in last]
    turns, sent = two_rotations(*summed(sums, "rows", [gram_work, order_first, order_rest]))
    came_turn = from_behind(sent, "cols", 1)
    own, cross, top = own_sums(chosen, kept["gram"], kept["split"], came[0], turns)
    meets, pair = came_sums(chosen, kept["split"], came, cross, top, turns)
    sums = second_sums(own, meets, pair, came_turn)

    second_turns, sent = two_rotations(*summed(sums, "rows", [turn_work, taken_work, moved_work]))
    behind_turn = from_behind(sent, "cols", -1)
    out = most_slots(chosen, kept["turned"], kept["moved"], second_turns)
    return last_slot(kept["turned"], kept["behind"], behind_turn, out)


def solution(mesh):
    placed = (P(("rows", "cols"), None, None), P("rows"), P())
    return jax.shard_map(
        body, mesh=mesh, in_specs=placed, out_specs=P("rows", "cols"), check_vma=False
    )
```

```python
import functools

import jax
import jax.numpy as jnp
from jax import lax
from jax.experimental import pallas as pl
from jax.experimental.pallas import tpu as pltpu
from jax.sharding import PartitionSpec as P

STEPS = 2
NS_STEPS = 6
SLOTS = 4
LANES = 128
WAYS = 2
PARTS = 8
MIB = 1024 * 1024

F32 = jnp.float32
BF16 = jnp.bfloat16
NN = (((1,), (0,)), ((), ()))
NT = (((1,), (1,)), ((), ()))
TN = (((0,), (0,)), ((), ()))

ANY = pl.BlockSpec(memory_space=pl.ANY)
HBM = pl.BlockSpec(memory_space=pltpu.HBM)
SMEM = pl.BlockSpec(memory_space=pltpu.SMEM)
VMEM = pl.BlockSpec(memory_space=pltpu.VMEM)


def pair_slots(chosen):
    partner = 2 - chosen
    low = jnp.where(partner == 0, 1, 0)
    high = jnp.where(partner == 2, 1, 2)
    return partner, low, high


def params(mib, flops=0, moved=0):
    return dict(
        compiler_params=pltpu.CompilerParams(vmem_limit_bytes=mib * MIB),
        cost_estimate=pl.CostEstimate(flops=int(flops), bytes_accessed=int(moved), transcendentals=0),
    )


def like(*arrays):
    return [jax.ShapeDtypeStruct(a.shape, a.dtype) for a in arrays]


def halves(value):
    high = value.astype(BF16)
    return high, (value - high.astype(F32)).astype(BF16)


def thirds(value):
    high = value.astype(BF16)
    rest = value - high.astype(F32)
    middle = rest.astype(BF16)
    return high, middle, (rest - middle.astype(F32)).astype(BF16)


def mul(a, b, dims=NN):
    return lax.dot_general(a, b, dims, preferred_element_type=F32)


def mul_split(a, b, dims=NN):
    return mul(a[0], b[0], dims) + (mul(a[0], b[1], dims) + mul(a[1], b[0], dims))


def dot_split(a, b, dims=NN):
    return mul_split(halves(a), halves(b), dims)


def identity(size):
    return lax.broadcasted_iota(jnp.int32, (size, size), 0) == lax.broadcasted_iota(jnp.int32, (size, size), 1)


def span(index, width):
    return pl.ds(pl.multiple_of(index * width, width), width)


def spread_kernel(tracks_ref, pieces_ref, came_ref, ready_ref, in_sems, out_sems):
    row_devices, frames, _, rows = came_ref.shape
    loads = [
        pltpu.make_async_copy(tracks_ref.at[:, :, pl.ds(r * rows, rows)], came_ref.at[r], in_sems.at[r])
        for r in range(row_devices)
    ]
    stores = [
        pltpu.make_async_copy(ready_ref.at[r], pieces_ref.at[r], out_sems.at[r]) for r in range(row_devices)
    ]
    for load in loads:
        load.start()
    for r in range(row_devices):
        loads[r].wait()
        for component in range(2):
            plane = came_ref[r, :, component, :]
            for group in range(frames // 8):
                for half in range(2):
                    ready_ref[r, 2 * component + half, 4 * group:4 * group + 4, :] = plane[
                        8 * group + 4 * half:8 * group + 4 * half + 4, :]
        stores[r].start()
    for store in stores:
        store.wait()


def spread(tracks, row_devices):
    frames, _, pixels = tracks.shape
    rows = pixels // row_devices
    shape = (row_devices, 4, frames // 2, rows)
    return pl.pallas_call(
        spread_kernel,
        in_specs=[ANY],
        out_specs=HBM,
        out_shape=jax.ShapeDtypeStruct(shape, F32),
        scratch_shapes=[
            pltpu.VMEM((row_devices, frames, 2, rows), F32),
            pltpu.VMEM(shape, F32),
            pltpu.SemaphoreType.DMA((row_devices,)),
            pltpu.SemaphoreType.DMA((row_devices,)),
        ],
        name="spread",
        **params(61, 0, 8 * tracks.size),
    )(tracks)


def coupling_kernel(chosen_ref, held_ref, sums_ref, one_ref, two_ref, came_ref, sems):
    tiles = came_ref.shape[0]
    width = sums_ref.shape[1]
    loads = [
        pltpu.make_async_copy(held_ref.at[:, pl.ds(k * LANES, LANES)], came_ref.at[k], sems.at[k])
        for k in range(tiles)
    ]
    for load in loads:
        load.start()
    partner, first, second = pair_slots(chosen_ref[0])
    products = [jnp.zeros((2 * width, 2 * width), F32)] * 2
    squares = [jnp.zeros((width, LANES), F32)] * SLOTS
    for part in range(0, tiles, WAYS):
        here = range(part, part + WAYS)
        for k in here:
            loads[k].wait()
        for index, slots in enumerate(((partner, SLOTS - 1), (first, second))):
            both = []
            for side, slot in enumerate(slots):
                pieces = [came_ref[k, pl.ds(slot, width, SLOTS), :] for k in here]
                for piece in pieces:
                    squares[2 * index + side] += piece * piece
                block = jnp.concatenate(pieces, axis=1)
                if index == 0:
                    half, place = divmod(part, tiles // 2)
                    (one_ref, two_ref)[half][
                        side * width:(side + 1) * width, place * LANES:(place + WAYS) * LANES] = block
                both.append(jnp.concatenate(halves(block), axis=0))
            products[index] += mul(both[0], both[1], NT)
    for index, product in enumerate(products):
        top = product[:width, :width] + (product[:width, width:] + product[width:, :width])
        sums_ref[index * width:(index + 1) * width, :] = top + product[width:, width:]
    rows = [jnp.sum(squared.T, axis=0, keepdims=True) for squared in squares]
    sums_ref[2 * width:, :] = jnp.concatenate(rows + [jnp.zeros((4, width), F32)], axis=0)


def couplings(chosen, held):
    columns, rows = held.shape
    width = columns // SLOTS
    return pl.pallas_call(
        coupling_kernel,
        in_specs=[SMEM, ANY],
        out_specs=[VMEM] * 4,
        out_shape=[
            jax.ShapeDtypeStruct((2 * width + 8, width), F32),
            jax.ShapeDtypeStruct((2 * width, rows // 2), F32),
            jax.ShapeDtypeStruct((2 * width, rows // 2), F32),
            jax.ShapeDtypeStruct((rows // LANES, columns, LANES), F32),
        ],
        scratch_shapes=[pltpu.SemaphoreType.DMA((rows // LANES,))],
        name="couplings",
        **params(16, 16 * width * width * rows, 6 * held.size),
    )(chosen, held)


def gram_kernel(value_ref, came_ref, carried_ref, gram_ref, split_ref):
    tiles = came_ref.shape[0]
    columns = gram_ref.shape[0]
    width = columns // SLOTS
    carried_ref[...] = value_ref[...]
    cross = 0.0
    for half in range(2):
        here = range(half * tiles // 2, (half + 1) * tiles // 2)
        for k in here:
            for slot in range(SLOTS):
                high, low = halves(came_ref[k, pl.ds(slot, width, SLOTS), :])
                lanes = slice(k * LANES, (k + 1) * LANES)
                split_ref[slot * width:(slot + 1) * width, lanes] = high
                split_ref[columns + slot * width:columns + (slot + 1) * width, lanes] = low
        lanes = slice(here.start * LANES, here.stop * LANES)
        high = split_ref[:columns, lanes]
        cross += mul(high, split_ref[columns:, lanes], NT)
        if half == 0:
            gram_ref[...] = mul(high, high, NT)
        else:
            gram_ref[...] += mul(high, high, NT) + (cross + cross.T)


def local_gram(value, came):
    tiles, columns, lanes = came.shape
    rows = tiles * lanes
    return pl.pallas_call(
        gram_kernel,
        in_specs=[VMEM] * 2,
        out_specs=[VMEM] * 3,
        out_shape=like(value) + [
            jax.ShapeDtypeStruct((columns, columns), F32),
            jax.ShapeDtypeStruct((2 * columns, rows), BF16),
        ],
        name="gram",
        **params(16, 4 * columns * columns * rows, 8 * columns * rows),
    )(value, came)


def left_terms(value):
    high, middle, low = thirds(value)
    return jnp.concatenate([high, middle], axis=1), jnp.concatenate([low, high], axis=1)


def right_terms(value):
    high, middle, low = thirds(value)
    wide = jnp.concatenate([high, middle], axis=1)
    return jnp.concatenate([wide, wide], axis=0), jnp.concatenate([high, low], axis=0)


def terms_product(left, right):
    width = right[1].shape[1]
    wide = mul(left[0], right[0])
    return wide[:, :width] + (wide[:, width:] + mul(left[1], right[1]))


def rotations(grams):
    width = grams[0][0].shape[0]
    eye = identity(width).astype(F32)
    couplings, scales, squares, products, crossed = [], [], [], [], []
    for block, row_sums, column_sums in grams:
        coupling = block / (jnp.broadcast_to(row_sums, (width, width)).T + column_sums)
        total = 1.0 + jnp.sum(coupling * coupling)
        couplings.append(coupling)
        flipped = coupling.T
        for one, two in ((coupling, flipped), (flipped, coupling)):
            scales.append(1.0 / jnp.sqrt(total))
            squares.append((eye + terms_product(left_terms(one), right_terms(two))) * (1.0 / total))
    for count in range(NS_STEPS):
        factors = [1.5 * eye - 0.5 * square for square in squares]
        rights = [right_terms(factor) for factor in factors]
        if count + 1 == NS_STEPS:
            crossed = [
                terms_product(left_terms(product), right_terms(coupling))
                for product, coupling in zip(products[::2], couplings)
            ]
        last = count + 1 == NS_STEPS
        if count == 0:
            products = [scale * factor for scale, factor in zip(scales, factors)]
        elif last:
            products = [terms_product(left_terms(product), right) for product, right in zip(products, rights)]
        else:
            both = [jnp.concatenate([square, product], axis=0) for square, product in zip(squares, products)]
            both = [terms_product(left_terms(one), right) for one, right in zip(both, rights)]
            squares, products = [one[:width] for one in both], [one[width:] for one in both]
        if count == 0:
            squares = [terms_product(left_terms(square), right) for square, right in zip(squares, rights)]
        if not last:
            squares = [terms_product(left_terms(square), right) for square, right in zip(squares, rights)]
    results = []
    for index, half in enumerate(crossed):
        across = terms_product(left_terms(factors[2 * index]), right_terms(half))
        results.append((products[2 * index], across, -across.T, products[2 * index + 1]))
    return results


def put_rotations(grams, rotation_ref, sent_ref):
    width = sent_ref.shape[1]
    for index, (top, right, bottom, end) in enumerate(rotations(grams)):
        rotation_ref[index, :width, :width] = top
        rotation_ref[index, :width, width:] = right
        rotation_ref[index, width:, :width] = bottom
        rotation_ref[index, width:, width:] = end
        if index == 0:
            sent_ref[:width, :] = right
            sent_ref[width:, :] = end


def rotation_kernel(one_ref, two_ref, rotation_ref, sent_ref):
    width = one_ref.shape[1]
    total = one_ref[...] + two_ref[...]
    sums = total[2 * width:]
    put_rotations(
        [(total[:width], sums[0:1], sums[1:2]), (total[width:2 * width], sums[2:3], sums[3:4])], rotation_ref, sent_ref)


def two_rotations(one, two):
    width = one.shape[1]
    return pl.pallas_call(
        rotation_kernel,
        in_specs=[VMEM] * 2,
        out_specs=[VMEM] * 2,
        out_shape=[
            jax.ShapeDtypeStruct((2, 2 * width, 2 * width), F32),
            jax.ShapeDtypeStruct((2 * width, width), F32),
        ],
        name="rotations",
        **params(16, 300 * 4 * width**3, 16 * width * width),
    )(one, two)


def places(chosen_ref, rotation_ref):
    width = rotation_ref.shape[1] // 2
    partner, first, second = pair_slots(chosen_ref[0])

    def place(slot):
        in_last = slot == partner
        members = (jnp.where(in_last, partner, first), jnp.where(in_last, SLOTS - 1, second))
        side = jnp.where(jnp.logical_or(in_last, slot == first), 0, 1)
        return members, rotation_ref[jnp.where(in_last, 0, 1), :, span(side, width)]

    return [place(slot) for slot in pair_slots(chosen_ref[1])]


def products_with(met, came):
    width = met[0].shape[0]
    by_high = mul(jnp.concatenate([*met, came[0]], axis=0), came[0], NT)
    by_low = mul(jnp.concatenate([met[0], came[0]], axis=0), came[1], NT)
    twice = by_low[width:]
    return by_high[:width] + (by_high[width:2 * width] + by_low[:width]), by_high[2 * width:] + (twice + twice.T)


def meet_kernel(chosen_ref, gram_ref, split_ref, came_ref, rotation_ref, _, sums_ref, met_ref, cross_ref, pair_ref):
    width = met_ref.shape[1]
    half = came_ref.shape[1]

    def between(rows, others):
        return jnp.concatenate(
            [jnp.concatenate([gram_ref[span(r, width), span(c, width)] for c in others], axis=1) for r in rows], axis=0)

    def squares(members, turn):
        return jnp.sum(turn * dot_split(between(members, members), turn), axis=0, keepdims=True)

    meets, low, high = places(chosen_ref, rotation_ref)
    here = [jnp.concatenate([split_ref[span(m + start, width), :] for m in meets[0]], axis=0) for start in (0, SLOTS)]
    met = halves(mul_split(halves(meets[1]), here, TN))
    for term in range(2):
        met_ref[term] = met[term]
    sums_ref[:width, :] = dot_split(low[1], dot_split(between(low[0], high[0]), high[1]), TN)
    sums_ref[width:, :] = jnp.concatenate(
        [squares(*meets), jnp.zeros((1, width), F32), squares(*low), squares(*high), jnp.zeros((4, width), F32)], axis=0)
    cross_ref[...], pair_ref[...] = products_with([part[:, :half] for part in met], halves(came_ref[...]))


def meet(chosen, gram, split, came, turns, after):
    pair, half = came.shape
    width = pair // 2
    return pl.pallas_call(
        meet_kernel,
        in_specs=[SMEM] + [VMEM] * 4 + [ANY],
        out_specs=[VMEM] * 4,
        out_shape=[
            jax.ShapeDtypeStruct((width + 8, width), F32),
            jax.ShapeDtypeStruct((2, width, 2 * half), BF16),
            jax.ShapeDtypeStruct((width, pair), F32),
            jax.ShapeDtypeStruct((pair, pair), F32),
        ],
        name="meet",
        **params(16, 64 * width * width * half, 30 * width * half),
    )(chosen, gram, split, came, turns, after)


def came_kernel(met_ref, came_ref, cross_ref, pair_ref, turn_ref, own_ref, sums_ref):
    width, half = met_ref.shape[1], came_ref.shape[1]
    cross, pair = products_with([met_ref[term, :, half:] for term in range(2)], halves(came_ref[...]))
    turn = turn_ref[...]
    split = halves(turn)
    sums_ref[:width, :] = mul_split(halves(cross + cross_ref[...]), split)
    squares = jnp.sum(turn * mul_split(halves(pair + pair_ref[...]), split), axis=0, keepdims=True)
    sums_ref[width:, :] = own_ref[...]
    sums_ref[2 * width + 1:2 * width + 2, :] = squares


def came_sums(met, came, cross, pair, came_turn, own):
    width = met.shape[1]
    return pl.pallas_call(
        came_kernel,
        in_specs=[VMEM] * 6,
        out_specs=VMEM,
        out_shape=jax.ShapeDtypeStruct((2 * width + 8, width), F32),
        name="came_sums",
        **params(16, 32 * width * came.size, 12 * came.size),
    )(met, came, cross, pair, came_turn, own)


def picks_kernel(order_ref, value_ref, carried_ref, picks_ref):
    rows = order_ref.shape[1]
    carried_ref[...] = value_ref[...]
    for start in range(0, rows, LANES):
        here = slice(start, start + LANES)
        place = jnp.broadcast_to(order_ref[:, here], (LANES, LANES)).T
        for lane in range(0, rows, LANES):
            lanes = lane + lax.broadcasted_iota(jnp.int32, (LANES, LANES), 1)
            picks_ref[here, lane:lane + LANES] = jnp.where(place == lanes, 1.0, 0.0).astype(BF16)


def picked(order, value):
    rows = order.shape[1]
    return pl.pallas_call(
        picks_kernel,
        in_specs=[VMEM] * 2,
        out_specs=[VMEM] * 2,
        out_shape=like(value) + [jax.ShapeDtypeStruct((rows, rows), BF16)],
        name="picks",
        **params(8, rows * rows, 2 * rows * rows),
    )(order, value)


def order_kernel(start, stop, picks_ref, split_ref, value_ref, *refs):
    carried_ref, matrix_ref = refs[-2:]
    width = matrix_ref.shape[3]
    carried_ref[...] = value_ref[...]
    both = mul(picks_ref[start:stop, :], split_ref[...], NT)
    for term in range(2):
        for block in range(SLOTS):
            first = (term * SLOTS + block) * width
            matrix_ref[term, block, start:stop, :] = both[:, first:first + width].astype(BF16)


def ordered(picks, split, value, span_of, into=None):
    columns, rows = split.shape[0] // 2, split.shape[1]
    extra = () if into is None else (into,)
    return pl.pallas_call(
        functools.partial(order_kernel, *span_of),
        in_specs=[VMEM] * (3 + len(extra)),
        out_specs=[VMEM] * 2,
        out_shape=like(value) + [jax.ShapeDtypeStruct((2, SLOTS, rows, columns // SLOTS), BF16)],
        input_output_aliases={} if into is None else {3: 1},
        name="row_order",
        **params(16, 4 * columns * rows * (span_of[1] - span_of[0]), 8 * columns * rows),
    )(picks, split, value, *extra)


def behind_kernel(chosen_ref, matrix_ref, rotation_ref, block_ref):
    rows, width = block_ref.shape
    (one, two), turn = places(chosen_ref, rotation_ref)[0]
    high, low = halves(turn)
    wide = jnp.concatenate([high, low], axis=1)
    chunk = rows // PARTS
    for part in range(PARTS):
        here = pl.ds(part * chunk, chunk)
        pair = [
            jnp.concatenate([matrix_ref[term, one, here], matrix_ref[term, two, here]], axis=1) for term in range(2)
        ]
        both = mul(pair[0], wide)
        block_ref[here] = both[:, :width] + (both[:, width:] + mul(pair[1], high))


def behind_block(chosen, matrix, turns):
    _, _, rows, width = matrix.shape
    return pl.pallas_call(
        behind_kernel,
        in_specs=[SMEM] + [VMEM] * 2,
        out_specs=VMEM,
        out_shape=jax.ShapeDtypeStruct((rows, width), F32),
        name="behind_block",
        **params(16, 12 * rows * width * width, 2 * matrix.size),
    )(chosen, matrix, turns)


def turn_kernel(chosen_ref, matrix_ref, rotation_ref, value_ref, carried_ref, turned_ref):
    rows, width = matrix_ref.shape[2:]
    partner, first, second = pair_slots(chosen_ref[0])
    carried_ref[...] = value_ref[...]
    chunk = rows // PARTS
    for index, (one, two) in enumerate(((partner, SLOTS - 1), (first, second))):
        turn = halves(rotation_ref[index])
        for part in range(PARTS):
            here = pl.ds(part * chunk, chunk)
            pair = [
                jnp.concatenate([matrix_ref[term, one, here], matrix_ref[term, two, here]], axis=1) for term in range(2)
            ]
            for term, half in enumerate(halves(mul_split(pair, turn))):
                turned_ref[term, one, here] = half[:, :width]
                turned_ref[term, two, here] = half[:, width:]

def turn(chosen, matrix, turns, value):
    _, _, rows, width = matrix.shape
    return pl.pallas_call(
        turn_kernel,
        in_specs=[SMEM] + [VMEM] * 3,
        out_specs=[VMEM] * 2,
        out_shape=like(value, matrix),
        name="first_turn",
        **params(16, 24 * rows * width * width, 4 * matrix.size),
    )(chosen, matrix, turns, value)


def moved_kernel(picks_ref, one_ref, two_ref, turn_ref, value_ref, carried_ref, block_ref):
    width = block_ref.shape[2]
    carried_ref[...] = value_ref[...]
    came = jnp.concatenate([one_ref[...], two_ref[...]], axis=1)
    both = mul(picks_ref[...], jnp.concatenate(halves(dot_split(turn_ref[...], came, TN)), axis=0), NT)
    for term in range(2):
        block_ref[term] = both[:, term * width:(term + 1) * width].astype(BF16)


def moved_block(picks, came, came_turn, value):
    rows = picks.shape[0]
    pair, width = came_turn.shape
    return pl.pallas_call(
        moved_kernel,
        in_specs=[VMEM] * 5,
        out_specs=[VMEM] * 2,
        out_shape=like(value) + [jax.ShapeDtypeStruct((2, rows, width), BF16)],
        name="moved_block",
        **params(16, 4 * width * rows * rows, 2 * picks.size),
    )(picks, *came, came_turn, value)


def most_kernel(chosen_ref, turned_ref, moved_ref, rotation_ref, out_ref, ready_ref, sems):
    rows, width = moved_ref.shape[1:]
    meets, low, high = pair_slots(chosen_ref[1])
    chunk = rows // PARTS
    pair_turn = halves(rotation_ref[1])
    meets_turn = halves(rotation_ref[0, :, :width])
    stores = []
    for part in range(PARTS):
        here = pl.ds(part * chunk, chunk)

        def beside(one, two):
            return [jnp.concatenate([one[term], two[term]], axis=1) for term in range(2)]

        def block(slot, here=here):
            return [turned_ref[term, slot, here] for term in range(2)]

        pair = mul_split(beside(block(low), block(high)), pair_turn)
        ready_ref[here, span(low, width)] = pair[:, :width]
        ready_ref[here, span(high, width)] = pair[:, width:]
        ready_ref[here, span(meets, width)] = mul_split(
            beside(block(meets), [moved_ref[term, here] for term in range(2)]), meets_turn)
        stores.append(pltpu.make_async_copy(
            ready_ref.at[here], out_ref.at[here, pl.ds(0, (SLOTS - 1) * width)], sems.at[part]))
        stores[-1].start()
    for store in stores:
        store.wait()


def most_slots(chosen, turned, moved, turns):
    _, _, rows, width = turned.shape
    return pl.pallas_call(
        most_kernel,
        in_specs=[SMEM] + [VMEM] * 3,
        out_specs=ANY,
        out_shape=jax.ShapeDtypeStruct((rows, SLOTS * width), F32),
        scratch_shapes=[pltpu.VMEM((rows, (SLOTS - 1) * width), F32), pltpu.SemaphoreType.DMA((PARTS,))],
        name="second_turn",
        **params(16, 18 * rows * width * width, 4 * turned.size),
    )(chosen, turned, moved, turns)


def rest_kernel(turned_ref, behind_ref, turn_ref, _, out_ref, ready_ref, sems):
    rows, width = behind_ref.shape
    chunk = rows // PARTS
    split = halves(turn_ref[...])
    stores = []
    for part in range(PARTS):
        here = pl.ds(part * chunk, chunk)
        pair = [
            jnp.concatenate([one, turned_ref[term, SLOTS - 1, here]], axis=1)
            for term, one in enumerate(halves(behind_ref[here]))
        ]
        ready_ref[here] = mul_split(pair, split)
        stores.append(pltpu.make_async_copy(
            ready_ref.at[here], out_ref.at[here, pl.ds((SLOTS - 1) * width, width)], sems.at[part]))
        stores[-1].start()
    for store in stores:
        store.wait()


def last_slot(turned, behind, behind_turn, out):
    _, _, rows, width = turned.shape
    return pl.pallas_call(
        rest_kernel,
        in_specs=[VMEM] * 3 + [ANY],
        out_specs=ANY,
        out_shape=like(out)[0],
        scratch_shapes=[pltpu.VMEM((rows, width), F32), pltpu.SemaphoreType.DMA((PARTS,))],
        input_output_aliases={3: 0},
        name="last_slot",
        **params(16, 12 * rows * width * width, 12 * rows * width),
    )(turned, behind, behind_turn, out)


def from_behind(value, axis, steps):
    count = lax.axis_size(axis)
    pairs = [(source, (source + steps) % count) for source in range(count)]
    return lax.ppermute(value, axis, pairs)


def summed(value, axis, beside):
    count = lax.axis_size(axis)
    got = jnp.zeros_like(value)
    if count & (count - 1):
        value, count = lax.psum(value, axis), 1
    distance = 1
    while distance < count:
        if distance > 1:
            value = value + got
        got = lax.ppermute(value, axis, [(source, source ^ distance) for source in range(count)])
        if beside:
            value = beside.pop(0)(value)
        distance *= 2
    for work in beside:
        value = work(value)
    return value, got


def body(tracks, pixel_order, pairing):
    frames_dev, _, pixel_total = tracks.shape
    row_devices = lax.axis_size("rows")
    row_count = pixel_total // row_devices
    pieces = spread(tracks, row_devices).reshape(row_devices * 4, frames_dev // 2, row_count)
    arrived = lax.all_to_all(pieces, ("rows", "cols"), split_axis=0, concat_axis=0, tiled=True)
    held = arrived.reshape(-1, row_count)
    order = (pixel_order - lax.axis_index("rows") * row_count).reshape(1, row_count)
    chosen = lax.dynamic_index_in_dim(pairing, lax.axis_index("cols"), axis=1, keepdims=False)
    part = row_count * 3 // 8
    kept = {}

    def gram_work(value):
        value, kept["gram"], kept["split"] = local_gram(value, tiles)
        return value

    def order_first(value):
        value, kept["picks"] = picked(order, value)
        value, kept["matrix"] = ordered(kept["picks"], kept["split"], value, (0, part))
        return value

    def order_rest(value):
        value, kept["matrix"] = ordered(kept["picks"], kept["split"], value, (part, row_count), kept["matrix"])
        return value

    def turn_work(value):
        value, kept["turned"] = turn(chosen, kept["matrix"], turns, value)
        return value

    def moved_work(value):
        value, kept["moved"] = moved_block(kept["picks"], came, came_turn, value)
        return value

    sums, *last, tiles = couplings(chosen, held)
    came = [from_behind(half, "cols", 1) for half in last]
    turns, sent = two_rotations(*summed(sums, "rows", [gram_work, order_first, order_rest]))
    came_turn = from_behind(sent, "cols", 1)
    behind_sent = behind_block(chosen, kept["matrix"], turns)
    behind = from_behind(behind_sent, "cols", -1)
    own, met, cross, pair = meet(chosen, kept["gram"], kept["split"], came[0], turns, behind_sent)
    sums = came_sums(met, came[1], cross, pair, came_turn, own)

    second_turns, sent = two_rotations(*summed(sums, "rows", [turn_work, moved_work]))
    behind_turn = from_behind(sent, "cols", -1)
    out = most_slots(chosen, kept["turned"], kept["moved"], second_turns)
    return last_slot(kept["turned"], behind, behind_turn, out)


def solution(mesh):
    placed = (P(("rows", "cols"), None, None), P("rows"), P())
    return jax.shard_map(
        body, mesh=mesh, in_specs=placed, out_specs=P("rows", "cols"), check_vma=False
    )
```

```python
import functools

import jax
import jax.numpy as jnp
from jax import lax
from jax.experimental import pallas as pl
from jax.experimental.pallas import tpu as pltpu
from jax.sharding import PartitionSpec as P

STEPS = 2
NS_STEPS = 6
SLOTS = 4
LANES = 128
WAYS = 2
PARTS = 8
MIB = 1024 * 1024

F32 = jnp.float32
BF16 = jnp.bfloat16
NN = (((1,), (0,)), ((), ()))
NT = (((1,), (1,)), ((), ()))
TN = (((0,), (0,)), ((), ()))

ANY = pl.BlockSpec(memory_space=pl.ANY)
HBM = pl.BlockSpec(memory_space=pltpu.HBM)
SMEM = pl.BlockSpec(memory_space=pltpu.SMEM)
VMEM = pl.BlockSpec(memory_space=pltpu.VMEM)


def pair_slots(chosen):
    partner = 2 - chosen
    low = jnp.where(partner == 0, 1, 0)
    high = jnp.where(partner == 2, 1, 2)
    return partner, low, high


def params(mib, flops=0, moved=0):
    return dict(
        compiler_params=pltpu.CompilerParams(vmem_limit_bytes=mib * MIB),
        cost_estimate=pl.CostEstimate(flops=int(flops), bytes_accessed=int(moved), transcendentals=0),
    )


def like(*arrays):
    return [jax.ShapeDtypeStruct(a.shape, a.dtype) for a in arrays]


def halves(value):
    high = value.astype(BF16)
    return high, (value - high.astype(F32)).astype(BF16)


def thirds(value):
    high = value.astype(BF16)
    rest = value - high.astype(F32)
    middle = rest.astype(BF16)
    return high, middle, (rest - middle.astype(F32)).astype(BF16)


def mul(a, b, dims=NN):
    return lax.dot_general(a, b, dims, preferred_element_type=F32)


def mul_split(a, b, dims=NN):
    return mul(a[0], b[0], dims) + (mul(a[0], b[1], dims) + mul(a[1], b[0], dims))


def mul_narrow(a, b):
    width = b[0].shape[1]
    both = mul(a[0], jnp.concatenate(b, axis=1))
    return both[:, :width] + (both[:, width:] + mul(a[1], b[0]))


def dot_split(a, b, dims=NN):
    return mul_split(halves(a), halves(b), dims)


def identity(size):
    return lax.broadcasted_iota(jnp.int32, (size, size), 0) == lax.broadcasted_iota(jnp.int32, (size, size), 1)


def span(index, width):
    return pl.ds(pl.multiple_of(index * width, width), width)


def spread_kernel(tracks_ref, pieces_ref, came_ref, ready_ref, in_sems, out_sems):
    row_devices, frames, _, rows = came_ref.shape
    loads = [
        pltpu.make_async_copy(tracks_ref.at[:, :, pl.ds(r * rows, rows)], came_ref.at[r], in_sems.at[r])
        for r in range(row_devices)
    ]
    stores = [
        pltpu.make_async_copy(ready_ref.at[r], pieces_ref.at[r], out_sems.at[r]) for r in range(row_devices)
    ]
    for load in loads:
        load.start()
    for r in range(row_devices):
        loads[r].wait()
        for component in range(2):
            plane = came_ref[r, :, component, :]
            for group in range(frames // 8):
                for half in range(2):
                    ready_ref[r, 2 * component + half, 4 * group:4 * group + 4, :] = plane[
                        8 * group + 4 * half:8 * group + 4 * half + 4, :]
        stores[r].start()
    for store in stores:
        store.wait()


def spread(tracks, row_devices):
    frames, _, pixels = tracks.shape
    rows = pixels // row_devices
    shape = (row_devices, 4, frames // 2, rows)
    return pl.pallas_call(
        spread_kernel,
        in_specs=[ANY],
        out_specs=HBM,
        out_shape=jax.ShapeDtypeStruct(shape, F32),
        scratch_shapes=[
            pltpu.VMEM((row_devices, frames, 2, rows), F32),
            pltpu.VMEM(shape, F32),
            pltpu.SemaphoreType.DMA((row_devices,)),
            pltpu.SemaphoreType.DMA((row_devices,)),
        ],
        name="spread",
        **params(61, 0, 8 * tracks.size),
    )(tracks)


def coupling_kernel(chosen_ref, held_ref, sums_ref, one_ref, two_ref, came_ref, sems):
    tiles = came_ref.shape[0]
    width = sums_ref.shape[1]
    loads = [
        pltpu.make_async_copy(held_ref.at[:, pl.ds(k * LANES, LANES)], came_ref.at[k], sems.at[k])
        for k in range(tiles)
    ]
    for load in loads:
        load.start()
    partner, first, second = pair_slots(chosen_ref[0])
    products = [jnp.zeros((2 * width, 2 * width), F32)] * 2
    squares = [jnp.zeros((width, LANES), F32)] * SLOTS
    for part in range(0, tiles, WAYS):
        here = range(part, part + WAYS)
        for k in here:
            loads[k].wait()
        for index, slots in enumerate(((partner, SLOTS - 1), (first, second))):
            both = []
            for side, slot in enumerate(slots):
                pieces = [came_ref[k, pl.ds(slot, width, SLOTS), :] for k in here]
                for piece in pieces:
                    squares[2 * index + side] += piece * piece
                block = jnp.concatenate(pieces, axis=1)
                if index == 0:
                    half, place = divmod(part, tiles // 2)
                    (one_ref, two_ref)[half][
                        side * width:(side + 1) * width, place * LANES:(place + WAYS) * LANES] = block
                both.append(jnp.concatenate(halves(block), axis=0))
            products[index] += mul(both[0], both[1], NT)
    for index, product in enumerate(products):
        top = product[:width, :width] + (product[:width, width:] + product[width:, :width])
        sums_ref[index * width:(index + 1) * width, :] = top + product[width:, width:]
    rows = [jnp.sum(squared.T, axis=0, keepdims=True) for squared in squares]
    sums_ref[2 * width:, :] = jnp.concatenate(rows + [jnp.zeros((4, width), F32)], axis=0)


def couplings(chosen, held):
    columns, rows = held.shape
    width = columns // SLOTS
    return pl.pallas_call(
        coupling_kernel,
        in_specs=[SMEM, ANY],
        out_specs=[VMEM] * 4,
        out_shape=[
            jax.ShapeDtypeStruct((2 * width + 8, width), F32),
            jax.ShapeDtypeStruct((2 * width, rows // 2), F32),
            jax.ShapeDtypeStruct((2 * width, rows // 2), F32),
            jax.ShapeDtypeStruct((rows // LANES, columns, LANES), F32),
        ],
        scratch_shapes=[pltpu.SemaphoreType.DMA((rows // LANES,))],
        name="couplings",
        **params(16, 16 * width * width * rows, 6 * held.size),
    )(chosen, held)


def gram_kernel(value_ref, came_ref, carried_ref, gram_ref, split_ref):
    tiles = came_ref.shape[0]
    columns = gram_ref.shape[0]
    width = columns // SLOTS
    carried_ref[...] = value_ref[...]
    cross = 0.0
    for half in range(2):
        here = range(half * tiles // 2, (half + 1) * tiles // 2)
        for k in here:
            for slot in range(SLOTS):
                high, low = halves(came_ref[k, pl.ds(slot, width, SLOTS), :])
                lanes = slice(k * LANES, (k + 1) * LANES)
                split_ref[slot * width:(slot + 1) * width, lanes] = high
                split_ref[columns + slot * width:columns + (slot + 1) * width, lanes] = low
        lanes = slice(here.start * LANES, here.stop * LANES)
        high = split_ref[:columns, lanes]
        cross += mul(high, split_ref[columns:, lanes], NT)
        if half == 0:
            gram_ref[...] = mul(high, high, NT)
        else:
            gram_ref[...] += mul(high, high, NT) + (cross + cross.T)


def local_gram(value, came):
    tiles, columns, lanes = came.shape
    rows = tiles * lanes
    return pl.pallas_call(
        gram_kernel,
        in_specs=[VMEM] * 2,
        out_specs=[VMEM] * 3,
        out_shape=like(value) + [
            jax.ShapeDtypeStruct((columns, columns), F32),
            jax.ShapeDtypeStruct((2 * columns, rows), BF16),
        ],
        name="gram",
        **params(16, 4 * columns * columns * rows, 8 * columns * rows),
    )(value, came)


def left_terms(value):
    high, middle, low = thirds(value)
    return jnp.concatenate([high, middle], axis=1), jnp.concatenate([low, high], axis=1)


def right_terms(value):
    high, middle, low = thirds(value)
    wide = jnp.concatenate([high, middle], axis=1)
    return jnp.concatenate([wide, wide], axis=0), jnp.concatenate([high, low], axis=0)


def terms_product(left, right):
    width = right[1].shape[1]
    wide = mul(left[0], right[0])
    return wide[:, :width] + (wide[:, width:] + mul(left[1], right[1]))


def rotations(grams):
    width = grams[0][0].shape[0]
    eye = identity(width).astype(F32)
    couplings, scales, squares, products, crossed = [], [], [], [], []
    for block, row_sums, column_sums in grams:
        coupling = block / (jnp.broadcast_to(row_sums, (width, width)).T + column_sums)
        total = 1.0 + jnp.sum(coupling * coupling)
        couplings.append(coupling)
        flipped = coupling.T
        for one, two in ((coupling, flipped), (flipped, coupling)):
            scales.append(1.0 / jnp.sqrt(total))
            squares.append((eye + terms_product(left_terms(one), right_terms(two))) * (1.0 / total))
    for count in range(NS_STEPS):
        factors = [1.5 * eye - 0.5 * square for square in squares]
        rights = [right_terms(factor) for factor in factors]
        if count + 1 == NS_STEPS:
            crossed = [
                terms_product(left_terms(product), right_terms(coupling))
                for product, coupling in zip(products[::2], couplings)
            ]
        last = count + 1 == NS_STEPS
        if count == 0:
            products = [scale * factor for scale, factor in zip(scales, factors)]
        elif last:
            products = [terms_product(left_terms(product), right) for product, right in zip(products, rights)]
        else:
            both = [jnp.concatenate([square, product], axis=0) for square, product in zip(squares, products)]
            both = [terms_product(left_terms(one), right) for one, right in zip(both, rights)]
            squares, products = [one[:width] for one in both], [one[width:] for one in both]
        if count == 0:
            squares = [terms_product(left_terms(square), right) for square, right in zip(squares, rights)]
        if not last:
            squares = [terms_product(left_terms(square), right) for square, right in zip(squares, rights)]
    results = []
    for index, half in enumerate(crossed):
        across = terms_product(left_terms(factors[2 * index]), right_terms(half))
        results.append((products[2 * index], across, -across.T, products[2 * index + 1]))
    return results


def put_rotations(grams, rotation_ref, sent_ref):
    width = sent_ref.shape[1]
    for index, (top, right, bottom, end) in enumerate(rotations(grams)):
        rotation_ref[index, :width, :width] = top
        rotation_ref[index, :width, width:] = right
        rotation_ref[index, width:, :width] = bottom
        rotation_ref[index, width:, width:] = end
        if index == 0:
            sent_ref[:width, :] = right
            sent_ref[width:, :] = end


def rotation_kernel(one_ref, two_ref, rotation_ref, sent_ref):
    width = one_ref.shape[1]
    total = one_ref[...] + two_ref[...]
    sums = total[2 * width:]
    put_rotations(
        [(total[:width], sums[0:1], sums[1:2]), (total[width:2 * width], sums[2:3], sums[3:4])], rotation_ref, sent_ref)


def later_kernel(one_ref, one_got_ref, two_ref, two_got_ref, rotation_ref, sent_ref):
    width = one_ref.shape[1]
    totals = one_ref[...] + one_got_ref[...], two_ref[...] + two_got_ref[...]
    put_rotations(
        [(total[:width], total[width:width + 1], total[width + 1:width + 2]) for total in totals], rotation_ref, sent_ref)


def two_rotations(*terms):
    width = terms[0].shape[1]
    return pl.pallas_call(
        rotation_kernel if len(terms) == 2 else later_kernel,
        in_specs=[VMEM] * len(terms),
        out_specs=[VMEM] * 2,
        out_shape=[
            jax.ShapeDtypeStruct((2, 2 * width, 2 * width), F32),
            jax.ShapeDtypeStruct((2 * width, width), F32),
        ],
        name="rotations",
        **params(16, 300 * 4 * width**3, 16 * width * width),
    )(*terms)


def places(chosen_ref, rotation_ref):
    width = rotation_ref.shape[1] // 2
    partner, first, second = pair_slots(chosen_ref[0])

    def place(slot):
        in_last = slot == partner
        members = (jnp.where(in_last, partner, first), jnp.where(in_last, SLOTS - 1, second))
        side = jnp.where(jnp.logical_or(in_last, slot == first), 0, 1)
        return members, rotation_ref[jnp.where(in_last, 0, 1), :, span(side, width)]

    return [place(slot) for slot in pair_slots(chosen_ref[1])]


def products_with(met, came):
    width = met[0].shape[0]
    by_high = mul(jnp.concatenate([*met, came[0]], axis=0), came[0], NT)
    by_low = mul(jnp.concatenate([met[0], came[0]], axis=0), came[1], NT)
    twice = by_low[width:]
    return by_high[:width] + (by_high[width:2 * width] + by_low[:width]), by_high[2 * width:] + (twice + twice.T)


def meet_kernel(chosen_ref, gram_ref, split_ref, came_ref, rotation_ref, _, sums_ref, met_ref, cross_ref, pair_ref):
    width = met_ref.shape[1]
    half = came_ref.shape[1]

    def between(rows, others):
        return jnp.concatenate(
            [jnp.concatenate([gram_ref[span(r, width), span(c, width)] for c in others], axis=1) for r in rows], axis=0)

    def squares(members, turn):
        return jnp.sum(turn * dot_split(between(members, members), turn), axis=0, keepdims=True)

    meets, low, high = places(chosen_ref, rotation_ref)
    here = [jnp.concatenate([split_ref[span(m + start, width), :] for m in meets[0]], axis=0) for start in (0, SLOTS)]
    turn = halves(meets[1])
    both = mul(jnp.concatenate(turn, axis=1), here[0], TN)
    met = halves(both[:width] + (both[width:] + mul(turn[0], here[1], TN)))
    for term in range(2):
        met_ref[term] = met[term]
    sums_ref[:width, :] = dot_split(low[1], dot_split(between(low[0], high[0]), high[1]), TN)
    sums_ref[width:, :] = jnp.concatenate(
        [squares(*low), squares(*high), squares(*meets), jnp.zeros((5, width), F32)], axis=0)
    cross_ref[...], pair_ref[...] = products_with([part[:, :half] for part in met], halves(came_ref[...]))


def meet(chosen, gram, split, came, turns, after):
    pair, half = came.shape
    width = pair // 2
    return pl.pallas_call(
        meet_kernel,
        in_specs=[SMEM] + [VMEM] * 4 + [ANY],
        out_specs=[VMEM] * 4,
        out_shape=[
            jax.ShapeDtypeStruct((width + 8, width), F32),
            jax.ShapeDtypeStruct((2, width, 2 * half), BF16),
            jax.ShapeDtypeStruct((width, pair), F32),
            jax.ShapeDtypeStruct((pair, pair), F32),
        ],
        name="meet",
        **params(16, 64 * width * width * half, 30 * width * half),
    )(chosen, gram, split, came, turns, after)


def came_kernel(met_ref, came_ref, cross_ref, pair_ref, turn_ref, own_ref, sums_ref):
    width, half = met_ref.shape[1], came_ref.shape[1]
    cross, pair = products_with([met_ref[term, :, half:] for term in range(2)], halves(came_ref[...]))
    turn = turn_ref[...]
    split = halves(turn)
    sums_ref[:width, :] = mul_split(halves(cross + cross_ref[...]), split)
    squares = jnp.sum(turn * mul_split(halves(pair + pair_ref[...]), split), axis=0, keepdims=True)
    sums_ref[width:, :] = jnp.concatenate([own_ref[width + 2:width + 3], squares, jnp.zeros((6, width), F32)], axis=0)


def came_sums(met, came, cross, pair, came_turn, own):
    width = met.shape[1]
    return pl.pallas_call(
        came_kernel,
        in_specs=[VMEM] * 6,
        out_specs=VMEM,
        out_shape=jax.ShapeDtypeStruct((width + 8, width), F32),
        name="came_sums",
        **params(16, 32 * width * came.size, 12 * came.size),
    )(met, came, cross, pair, came_turn, own)


def picks_kernel(order_ref, value_ref, carried_ref, picks_ref):
    rows = order_ref.shape[1]
    carried_ref[...] = value_ref[...]
    for start in range(0, rows, LANES):
        here = slice(start, start + LANES)
        place = jnp.broadcast_to(order_ref[:, here], (LANES, LANES)).T
        for lane in range(0, rows, LANES):
            lanes = lane + lax.broadcasted_iota(jnp.int32, (LANES, LANES), 1)
            picks_ref[here, lane:lane + LANES] = jnp.where(place == lanes, 1.0, 0.0).astype(BF16)


def picked(order, value):
    rows = order.shape[1]
    return pl.pallas_call(
        picks_kernel,
        in_specs=[VMEM] * 2,
        out_specs=[VMEM] * 2,
        out_shape=like(value) + [jax.ShapeDtypeStruct((rows, rows), BF16)],
        name="picks",
        **params(8, rows * rows, 2 * rows * rows),
    )(order, value)


def order_kernel(start, stop, picks_ref, split_ref, value_ref, *refs):
    carried_ref, matrix_ref = refs[-2:]
    width = matrix_ref.shape[3]
    carried_ref[...] = value_ref[...]
    both = mul(picks_ref[start:stop, :], split_ref[...], NT)
    for term in range(2):
        for block in range(SLOTS):
            first = (term * SLOTS + block) * width
            matrix_ref[term, block, start:stop, :] = both[:, first:first + width].astype(BF16)


def ordered(picks, split, value, span_of, into=None):
    columns, rows = split.shape[0] // 2, split.shape[1]
    extra = () if into is None else (into,)
    return pl.pallas_call(
        functools.partial(order_kernel, *span_of),
        in_specs=[VMEM] * (3 + len(extra)),
        out_specs=[VMEM] * 2,
        out_shape=like(value) + [jax.ShapeDtypeStruct((2, SLOTS, rows, columns // SLOTS), BF16)],
        input_output_aliases={} if into is None else {3: 1},
        name="row_order",
        **params(16, 4 * columns * rows * (span_of[1] - span_of[0]), 8 * columns * rows),
    )(picks, split, value, *extra)


def behind_kernel(chosen_ref, matrix_ref, rotation_ref, block_ref):
    rows, width = block_ref.shape
    (one, two), turn = places(chosen_ref, rotation_ref)[0]
    turn = halves(turn)
    chunk = rows // PARTS
    for part in range(PARTS):
        here = pl.ds(part * chunk, chunk)
        pair = [
            jnp.concatenate([matrix_ref[term, one, here], matrix_ref[term, two, here]], axis=1) for term in range(2)
        ]
        block_ref[here] = mul_narrow(pair, turn)


def behind_block(chosen, matrix, turns):
    _, _, rows, width = matrix.shape
    return pl.pallas_call(
        behind_kernel,
        in_specs=[SMEM] + [VMEM] * 2,
        out_specs=VMEM,
        out_shape=jax.ShapeDtypeStruct((rows, width), F32),
        name="behind_block",
        **params(16, 12 * rows * width * width, 2 * matrix.size),
    )(chosen, matrix, turns)


def turn_kernel(chosen_ref, matrix_ref, rotation_ref, value_ref, carried_ref, turned_ref):
    rows, width = matrix_ref.shape[2:]
    partner, first, second = pair_slots(chosen_ref[0])
    carried_ref[...] = value_ref[...]
    chunk = rows // PARTS
    for index, (one, two) in enumerate(((partner, SLOTS - 1), (first, second))):
        turn = halves(rotation_ref[index])
        for part in range(PARTS):
            here = pl.ds(part * chunk, chunk)
            pair = [
                jnp.concatenate([matrix_ref[term, one, here], matrix_ref[term, two, here]], axis=1) for term in range(2)
            ]
            for term, half in enumerate(halves(mul_split(pair, turn))):
                turned_ref[term, one, here] = half[:, :width]
                turned_ref[term, two, here] = half[:, width:]

def turn(chosen, matrix, turns, value):
    _, _, rows, width = matrix.shape
    return pl.pallas_call(
        turn_kernel,
        in_specs=[SMEM] + [VMEM] * 3,
        out_specs=[VMEM] * 2,
        out_shape=like(value, matrix),
        name="first_turn",
        **params(16, 24 * rows * width * width, 4 * matrix.size),
    )(chosen, matrix, turns, value)


def moved_kernel(picks_ref, one_ref, two_ref, turn_ref, value_ref, carried_ref, block_ref):
    width = block_ref.shape[2]
    carried_ref[...] = value_ref[...]
    came = jnp.concatenate([one_ref[...], two_ref[...]], axis=1)
    both = mul(picks_ref[...], jnp.concatenate(halves(dot_split(turn_ref[...], came, TN)), axis=0), NT)
    for term in range(2):
        block_ref[term] = both[:, term * width:(term + 1) * width].astype(BF16)


def moved_block(picks, came, came_turn, value):
    rows = picks.shape[0]
    pair, width = came_turn.shape
    return pl.pallas_call(
        moved_kernel,
        in_specs=[VMEM] * 5,
        out_specs=[VMEM] * 2,
        out_shape=like(value) + [jax.ShapeDtypeStruct((2, rows, width), BF16)],
        name="moved_block",
        **params(16, 4 * width * rows * rows, 2 * picks.size),
    )(picks, *came, came_turn, value)


def most_kernel(chosen_ref, turned_ref, moved_ref, rotation_ref, out_ref, ready_ref, sems):
    rows, width = moved_ref.shape[1:]
    meets, low, high = pair_slots(chosen_ref[1])
    chunk = rows // PARTS
    pair_turn = halves(rotation_ref[1])
    meets_turn = halves(rotation_ref[0, :, :width])
    stores = []
    for part in range(PARTS):
        here = pl.ds(part * chunk, chunk)

        def beside(one, two):
            return [jnp.concatenate([one[term], two[term]], axis=1) for term in range(2)]

        def block(slot, here=here):
            return [turned_ref[term, slot, here] for term in range(2)]

        pair = mul_split(beside(block(low), block(high)), pair_turn)
        ready_ref[here, span(low, width)] = pair[:, :width]
        ready_ref[here, span(high, width)] = pair[:, width:]
        ready_ref[here, span(meets, width)] = mul_narrow(
            beside(block(meets), [moved_ref[term, here] for term in range(2)]), meets_turn)
        stores.append(pltpu.make_async_copy(
            ready_ref.at[here], out_ref.at[here, pl.ds(0, (SLOTS - 1) * width)], sems.at[part]))
        stores[-1].start()
    for store in stores:
        store.wait()


def most_slots(chosen, turned, moved, turns):
    _, _, rows, width = turned.shape
    return pl.pallas_call(
        most_kernel,
        in_specs=[SMEM] + [VMEM] * 3,
        out_specs=ANY,
        out_shape=jax.ShapeDtypeStruct((rows, SLOTS * width), F32),
        scratch_shapes=[pltpu.VMEM((rows, (SLOTS - 1) * width), F32), pltpu.SemaphoreType.DMA((PARTS,))],
        name="second_turn",
        **params(16, 18 * rows * width * width, 4 * turned.size),
    )(chosen, turned, moved, turns)


def rest_kernel(turned_ref, behind_ref, turn_ref, _, out_ref, ready_ref, sems):
    rows, width = behind_ref.shape
    chunk = rows // PARTS
    split = halves(turn_ref[...])
    stores = []
    for part in range(PARTS):
        here = pl.ds(part * chunk, chunk)
        pair = [
            jnp.concatenate([one, turned_ref[term, SLOTS - 1, here]], axis=1)
            for term, one in enumerate(halves(behind_ref[here]))
        ]
        ready_ref[here] = mul_narrow(pair, split)
        stores.append(pltpu.make_async_copy(
            ready_ref.at[here], out_ref.at[here, pl.ds((SLOTS - 1) * width, width)], sems.at[part]))
        stores[-1].start()
    for store in stores:
        store.wait()


def last_slot(turned, behind, behind_turn, out):
    _, _, rows, width = turned.shape
    return pl.pallas_call(
        rest_kernel,
        in_specs=[VMEM] * 3 + [ANY],
        out_specs=ANY,
        out_shape=like(out)[0],
        scratch_shapes=[pltpu.VMEM((rows, width), F32), pltpu.SemaphoreType.DMA((PARTS,))],
        input_output_aliases={3: 0},
        name="last_slot",
        **params(16, 12 * rows * width * width, 12 * rows * width),
    )(turned, behind, behind_turn, out)


def from_behind(value, axis, steps):
    count = lax.axis_size(axis)
    pairs = [(source, (source + steps) % count) for source in range(count)]
    return lax.ppermute(value, axis, pairs)


def summed(value, axis, beside):
    count = lax.axis_size(axis)
    got = jnp.zeros_like(value)
    if count & (count - 1):
        value, count = lax.psum(value, axis), 1
    distance = 1
    while distance < count:
        if distance > 1:
            value = value + got
        got = lax.ppermute(value, axis, [(source, source ^ distance) for source in range(count)])
        if beside:
            value = beside.pop(0)(value)
        distance *= 2
    for work in beside:
        value = work(value)
    return value, got


def both_summed(one, two, axis, beside):
    count = lax.axis_size(axis)
    one, two = lax.optimization_barrier((one, two))
    values, got = [one, two], [jnp.zeros_like(one), jnp.zeros_like(two)]
    if count & (count - 1):
        values, count = [lax.psum(value, axis) for value in values], 1
    d = [1 << bit for bit in range(count.bit_length() - 1)]
    for place, distances in enumerate(zip(*(d[:1] + d[:0:-1], d[::-1]))):
        if place:
            values = [value + came for value, came in zip(values, got)]
        got = [
            lax.ppermute(value, axis, [(source, source ^ distance) for source in range(count)])
            for value, distance in zip(values, distances)
        ]
        if beside:
            values[0] = beside.pop(0)(values[0])
    for work in beside:
        values[0] = work(values[0])
    return values[0], got[0], values[1], got[1]


def body(tracks, pixel_order, pairing):
    frames_dev, _, pixel_total = tracks.shape
    row_devices = lax.axis_size("rows")
    row_count = pixel_total // row_devices
    pieces = spread(tracks, row_devices).reshape(row_devices * 4, frames_dev // 2, row_count)
    arrived = lax.all_to_all(pieces, ("rows", "cols"), split_axis=0, concat_axis=0, tiled=True)
    held = arrived.reshape(-1, row_count)
    order = (pixel_order - lax.axis_index("rows") * row_count).reshape(1, row_count)
    chosen = lax.dynamic_index_in_dim(pairing, lax.axis_index("cols"), axis=1, keepdims=False)
    part = row_count * 3 // 8
    kept = {}

    def gram_work(value):
        value, kept["gram"], kept["split"] = local_gram(value, tiles)
        return value

    def order_first(value):
        value, kept["picks"] = picked(order, value)
        value, kept["matrix"] = ordered(kept["picks"], kept["split"], value, (0, part))
        return value

    def order_rest(value):
        value, kept["matrix"] = ordered(kept["picks"], kept["split"], value, (part, row_count), kept["matrix"])
        return value

    def turn_work(value):
        value, kept["turned"] = turn(chosen, kept["matrix"], turns, value)
        return value

    def moved_work(value):
        value, kept["moved"] = moved_block(kept["picks"], came, came_turn, value)
        return value

    sums, *last, tiles = couplings(chosen, held)
    came = [from_behind(half, "cols", 1) for half in last]
    turns, sent = two_rotations(*summed(sums, "rows", [gram_work, order_first, order_rest]))
    came_turn = from_behind(sent, "cols", 1)
    behind_sent = behind_block(chosen, kept["matrix"], turns)
    own, met, cross, pair = meet(chosen, kept["gram"], kept["split"], came[0], turns, behind_sent)
    behind = from_behind(lax.optimization_barrier((behind_sent, came_turn, met))[0], "cols", -1)
    sums = came_sums(met, came[1], cross, pair, came_turn, own)

    second_turns, sent = two_rotations(*both_summed(sums, own, "rows", [turn_work, moved_work]))
    behind_turn = from_behind(sent, "cols", -1)
    out = most_slots(chosen, kept["turned"], kept["moved"], second_turns)
    return last_slot(kept["turned"], behind, behind_turn, out)


def solution(mesh):
    placed = (P(("rows", "cols"), None, None), P("rows"), P())
    return jax.shard_map(
        body, mesh=mesh, in_specs=placed, out_specs=P("rows", "cols"), check_vma=False
    )
```

```python
import functools

import jax
import jax.numpy as jnp
from jax import lax
from jax.experimental import pallas as pl
from jax.experimental.pallas import tpu as pltpu
from jax.sharding import PartitionSpec as P

STEPS = 2
NS_STEPS = 6
SLOTS = 4
LANES = 128
WAYS = 2
PARTS = 8
MIB = 1024 * 1024

F32 = jnp.float32
BF16 = jnp.bfloat16
NN = (((1,), (0,)), ((), ()))
NT = (((1,), (1,)), ((), ()))
TN = (((0,), (0,)), ((), ()))

ANY = pl.BlockSpec(memory_space=pl.ANY)
HBM = pl.BlockSpec(memory_space=pltpu.HBM)
SMEM = pl.BlockSpec(memory_space=pltpu.SMEM)
VMEM = pl.BlockSpec(memory_space=pltpu.VMEM)


def pair_slots(chosen):
    partner = 2 - chosen
    low = jnp.where(partner == 0, 1, 0)
    high = jnp.where(partner == 2, 1, 2)
    return partner, low, high


def params(mib, flops=0, moved=0):
    return dict(
        compiler_params=pltpu.CompilerParams(vmem_limit_bytes=mib * MIB),
        cost_estimate=pl.CostEstimate(flops=int(flops), bytes_accessed=int(moved), transcendentals=0),
    )


def like(*arrays):
    return [jax.ShapeDtypeStruct(a.shape, a.dtype) for a in arrays]


def halves(value):
    high = value.astype(BF16)
    return high, (value - high.astype(F32)).astype(BF16)


def thirds(value):
    high = value.astype(BF16)
    rest = value - high.astype(F32)
    middle = rest.astype(BF16)
    return high, middle, (rest - middle.astype(F32)).astype(BF16)


def mul(a, b, dims=NN):
    return lax.dot_general(a, b, dims, preferred_element_type=F32)


def mul_split(a, b, dims=NN):
    return mul(a[0], b[0], dims) + (mul(a[0], b[1], dims) + mul(a[1], b[0], dims))


def mul_narrow(a, b):
    width = b[0].shape[1]
    both = mul(a[0], jnp.concatenate(b, axis=1))
    return both[:, :width] + (both[:, width:] + mul(a[1], b[0]))


def dot_split(a, b, dims=NN):
    return mul_split(halves(a), halves(b), dims)


def identity(size):
    return lax.broadcasted_iota(jnp.int32, (size, size), 0) == lax.broadcasted_iota(jnp.int32, (size, size), 1)


def span(index, width):
    return pl.ds(pl.multiple_of(index * width, width), width)


def spread_kernel(tracks_ref, pieces_ref, came_ref, ready_ref, in_sems, out_sems):
    row_devices, frames, _, rows = came_ref.shape
    loads = [
        pltpu.make_async_copy(tracks_ref.at[:, :, pl.ds(r * rows, rows)], came_ref.at[r], in_sems.at[r])
        for r in range(row_devices)
    ]
    stores = [
        pltpu.make_async_copy(ready_ref.at[r], pieces_ref.at[r], out_sems.at[r]) for r in range(row_devices)
    ]
    for load in loads:
        load.start()
    for r in range(row_devices):
        loads[r].wait()
        for component in range(2):
            plane = came_ref[r, :, component, :]
            for group in range(frames // 8):
                for half in range(2):
                    ready_ref[r, 2 * component + half, 4 * group:4 * group + 4, :] = plane[
                        8 * group + 4 * half:8 * group + 4 * half + 4, :]
        stores[r].start()
    for store in stores:
        store.wait()


def spread(tracks, row_devices):
    frames, _, pixels = tracks.shape
    rows = pixels // row_devices
    shape = (row_devices, 4, frames // 2, rows)
    return pl.pallas_call(
        spread_kernel,
        in_specs=[ANY],
        out_specs=HBM,
        out_shape=jax.ShapeDtypeStruct(shape, F32),
        scratch_shapes=[
            pltpu.VMEM((row_devices, frames, 2, rows), F32),
            pltpu.VMEM(shape, F32),
            pltpu.SemaphoreType.DMA((row_devices,)),
            pltpu.SemaphoreType.DMA((row_devices,)),
        ],
        name="spread",
        **params(61, 0, 8 * tracks.size),
    )(tracks)


def coupling_kernel(chosen_ref, held_ref, sums_ref, one_ref, two_ref, came_ref, sems):
    tiles = came_ref.shape[0]
    width = sums_ref.shape[1]
    loads = [
        pltpu.make_async_copy(held_ref.at[:, pl.ds(k * LANES, LANES)], came_ref.at[k], sems.at[k])
        for k in range(tiles)
    ]
    for load in loads:
        load.start()
    partner, first, second = pair_slots(chosen_ref[0])
    products = [jnp.zeros((2 * width, 2 * width), F32)] * 2
    squares = [jnp.zeros((width, LANES), F32)] * SLOTS
    for part in range(0, tiles, WAYS):
        here = range(part, part + WAYS)
        for k in here:
            loads[k].wait()
        for index, slots in enumerate(((partner, SLOTS - 1), (first, second))):
            both = []
            for side, slot in enumerate(slots):
                pieces = [came_ref[k, pl.ds(slot, width, SLOTS), :] for k in here]
                for piece in pieces:
                    squares[2 * index + side] += piece * piece
                block = jnp.concatenate(pieces, axis=1)
                if index == 0:
                    half, place = divmod(part, tiles // 2)
                    (one_ref, two_ref)[half][
                        side * width:(side + 1) * width, place * LANES:(place + WAYS) * LANES] = block
                both.append(jnp.concatenate(halves(block), axis=0))
            products[index] += mul(both[0], both[1], NT)
    for index, product in enumerate(products):
        top = product[:width, :width] + (product[:width, width:] + product[width:, :width])
        sums_ref[index * width:(index + 1) * width, :] = top + product[width:, width:]
    rows = [jnp.sum(squared.T, axis=0, keepdims=True) for squared in squares]
    sums_ref[2 * width:, :] = jnp.concatenate(rows + [jnp.zeros((4, width), F32)], axis=0)


def couplings(chosen, held):
    columns, rows = held.shape
    width = columns // SLOTS
    return pl.pallas_call(
        coupling_kernel,
        in_specs=[SMEM, ANY],
        out_specs=[VMEM] * 4,
        out_shape=[
            jax.ShapeDtypeStruct((2 * width + 8, width), F32),
            jax.ShapeDtypeStruct((2 * width, rows // 2), F32),
            jax.ShapeDtypeStruct((2 * width, rows // 2), F32),
            jax.ShapeDtypeStruct((rows // LANES, columns, LANES), F32),
        ],
        scratch_shapes=[pltpu.SemaphoreType.DMA((rows // LANES,))],
        name="couplings",
        **params(16, 16 * width * width * rows, 6 * held.size),
    )(chosen, held)


def gram_kernel(value_ref, came_ref, carried_ref, gram_ref, split_ref):
    tiles = came_ref.shape[0]
    columns = gram_ref.shape[0]
    width = columns // SLOTS
    carried_ref[...] = value_ref[...]
    cross = 0.0
    for half in range(2):
        here = range(half * tiles // 2, (half + 1) * tiles // 2)
        for k in here:
            for slot in range(SLOTS):
                high, low = halves(came_ref[k, pl.ds(slot, width, SLOTS), :])
                lanes = slice(k * LANES, (k + 1) * LANES)
                split_ref[slot * width:(slot + 1) * width, lanes] = high
                split_ref[columns + slot * width:columns + (slot + 1) * width, lanes] = low
        lanes = slice(here.start * LANES, here.stop * LANES)
        high = split_ref[:columns, lanes]
        cross += mul(high, split_ref[columns:, lanes], NT)
        if half == 0:
            gram_ref[...] = mul(high, high, NT)
        else:
            gram_ref[...] += mul(high, high, NT) + (cross + cross.T)


def local_gram(value, came):
    tiles, columns, lanes = came.shape
    rows = tiles * lanes
    return pl.pallas_call(
        gram_kernel,
        in_specs=[VMEM] * 2,
        out_specs=[VMEM] * 3,
        out_shape=like(value) + [
            jax.ShapeDtypeStruct((columns, columns), F32),
            jax.ShapeDtypeStruct((2 * columns, rows), BF16),
        ],
        name="gram",
        **params(16, 4 * columns * columns * rows, 8 * columns * rows),
    )(value, came)


def left_terms(value):
    high, middle, low = thirds(value)
    return jnp.concatenate([high, middle], axis=1), jnp.concatenate([low, high], axis=1)


def right_terms(value):
    high, middle, low = thirds(value)
    wide = jnp.concatenate([high, middle], axis=1)
    return jnp.concatenate([wide, wide], axis=0), jnp.concatenate([high, low], axis=0)


def terms_product(left, right):
    width = right[1].shape[1]
    wide = mul(left[0], right[0])
    return wide[:, :width] + (wide[:, width:] + mul(left[1], right[1]))


def rotations(grams):
    width = grams[0][0].shape[0]
    eye = identity(width).astype(F32)
    couplings, scales, squares, products, crossed = [], [], [], [], []
    for block, row_sums, column_sums in grams:
        coupling = block / (jnp.broadcast_to(row_sums, (width, width)).T + column_sums)
        total = 1.0 + jnp.sum(coupling * coupling)
        couplings.append(coupling)
        flipped = coupling.T
        for one, two in ((coupling, flipped), (flipped, coupling)):
            scales.append(1.0 / jnp.sqrt(total))
            squares.append((eye + terms_product(left_terms(one), right_terms(two))) * (1.0 / total))
    for count in range(NS_STEPS):
        factors = [1.5 * eye - 0.5 * square for square in squares]
        rights = [right_terms(factor) for factor in factors]
        if count + 1 == NS_STEPS:
            crossed = [
                terms_product(left_terms(product), right_terms(coupling))
                for product, coupling in zip(products[::2], couplings)
            ]
        last = count + 1 == NS_STEPS
        if count == 0:
            products = [scale * factor for scale, factor in zip(scales, factors)]
        elif last:
            products = [terms_product(left_terms(product), right) for product, right in zip(products, rights)]
        else:
            both = [jnp.concatenate([square, product], axis=0) for square, product in zip(squares, products)]
            both = [terms_product(left_terms(one), right) for one, right in zip(both, rights)]
            squares, products = [one[:width] for one in both], [one[width:] for one in both]
        if count == 0:
            squares = [terms_product(left_terms(square), right) for square, right in zip(squares, rights)]
        if not last:
            squares = [terms_product(left_terms(square), right) for square, right in zip(squares, rights)]
    results = []
    for index, half in enumerate(crossed):
        across = terms_product(left_terms(factors[2 * index]), right_terms(half))
        results.append((products[2 * index], across, -across.T, products[2 * index + 1]))
    return results


def put_rotations(grams, rotation_ref, sent_ref):
    width = sent_ref.shape[1]
    for index, (top, right, bottom, end) in enumerate(rotations(grams)):
        rotation_ref[index, :width, :width] = top
        rotation_ref[index, :width, width:] = right
        rotation_ref[index, width:, :width] = bottom
        rotation_ref[index, width:, width:] = end
        if index == 0:
            sent_ref[:width, :] = right
            sent_ref[width:, :] = end


def rotation_kernel(one_ref, two_ref, rotation_ref, sent_ref):
    width = one_ref.shape[1]
    total = one_ref[...] + two_ref[...]
    sums = total[2 * width:]
    put_rotations(
        [(total[:width], sums[0:1], sums[1:2]), (total[width:2 * width], sums[2:3], sums[3:4])], rotation_ref, sent_ref)


def later_kernel(one_ref, one_got_ref, two_ref, two_got_ref, rotation_ref, sent_ref):
    width = one_ref.shape[1]
    totals = one_ref[...] + one_got_ref[...], two_ref[...] + two_got_ref[...]
    put_rotations(
        [(total[:width], total[width:width + 1], total[width + 1:width + 2]) for total in totals], rotation_ref, sent_ref)


def two_rotations(*terms):
    width = terms[0].shape[1]
    return pl.pallas_call(
        rotation_kernel if len(terms) == 2 else later_kernel,
        in_specs=[VMEM] * len(terms),
        out_specs=[VMEM] * 2,
        out_shape=[
            jax.ShapeDtypeStruct((2, 2 * width, 2 * width), F32),
            jax.ShapeDtypeStruct((2 * width, width), F32),
        ],
        name="rotations",
        **params(16, 300 * 4 * width**3, 16 * width * width),
    )(*terms)


def places(chosen_ref, rotation_ref):
    width = rotation_ref.shape[1] // 2
    partner, first, second = pair_slots(chosen_ref[0])

    def place(slot):
        in_last = slot == partner
        members = (jnp.where(in_last, partner, first), jnp.where(in_last, SLOTS - 1, second))
        side = jnp.where(jnp.logical_or(in_last, slot == first), 0, 1)
        return members, rotation_ref[jnp.where(in_last, 0, 1), :, span(side, width)]

    return [place(slot) for slot in pair_slots(chosen_ref[1])]


def products_with(met, came):
    width = met[0].shape[0]
    by_high = mul(jnp.concatenate([*met, came[0]], axis=0), came[0], NT)
    by_low = mul(jnp.concatenate([met[0], came[0]], axis=0), came[1], NT)
    twice = by_low[width:]
    return by_high[:width] + (by_high[width:2 * width] + by_low[:width]), by_high[2 * width:] + (twice + twice.T)


def meet_kernel(chosen_ref, gram_ref, split_ref, came_ref, rotation_ref, _, sums_ref, met_ref, cross_ref, pair_ref):
    width = met_ref.shape[1]
    half = came_ref.shape[1]

    def between(rows, others):
        return jnp.concatenate(
            [jnp.concatenate([gram_ref[span(r, width), span(c, width)] for c in others], axis=1) for r in rows], axis=0)

    def squares(members, turn):
        return jnp.sum(turn * dot_split(between(members, members), turn), axis=0, keepdims=True)

    meets, low, high = places(chosen_ref, rotation_ref)
    here = [jnp.concatenate([split_ref[span(m + start, width), :] for m in meets[0]], axis=0) for start in (0, SLOTS)]
    turn = halves(meets[1])
    both = mul(jnp.concatenate(turn, axis=1), here[0], TN)
    met = halves(both[:width] + (both[width:] + mul(turn[0], here[1], TN)))
    for term in range(2):
        met_ref[term] = met[term]
    sums_ref[:width, :] = dot_split(low[1], dot_split(between(low[0], high[0]), high[1]), TN)
    sums_ref[width:, :] = jnp.concatenate(
        [squares(*low), squares(*high), squares(*meets), jnp.zeros((5, width), F32)], axis=0)
    cross_ref[...], pair_ref[...] = products_with([part[:, :half] for part in met], halves(came_ref[...]))


def meet(chosen, gram, split, came, turns, after):
    pair, half = came.shape
    width = pair // 2
    return pl.pallas_call(
        meet_kernel,
        in_specs=[SMEM] + [VMEM] * 4 + [ANY],
        out_specs=[VMEM] * 4,
        out_shape=[
            jax.ShapeDtypeStruct((width + 8, width), F32),
            jax.ShapeDtypeStruct((2, width, 2 * half), BF16),
            jax.ShapeDtypeStruct((width, pair), F32),
            jax.ShapeDtypeStruct((pair, pair), F32),
        ],
        name="meet",
        **params(16, 64 * width * width * half, 30 * width * half),
    )(chosen, gram, split, came, turns, after)


def came_kernel(met_ref, came_ref, cross_ref, pair_ref, turn_ref, own_ref, sums_ref):
    width, half = met_ref.shape[1], came_ref.shape[1]
    cross, pair = products_with([met_ref[term, :, half:] for term in range(2)], halves(came_ref[...]))
    turn = turn_ref[...]
    split = halves(turn)
    sums_ref[:width, :] = mul_split(halves(cross + cross_ref[...]), split)
    squares = jnp.sum(turn * mul_split(halves(pair + pair_ref[...]), split), axis=0, keepdims=True)
    sums_ref[width:, :] = jnp.concatenate([own_ref[width + 2:width + 3], squares, jnp.zeros((6, width), F32)], axis=0)


def came_sums(met, came, cross, pair, came_turn, own):
    width = met.shape[1]
    return pl.pallas_call(
        came_kernel,
        in_specs=[VMEM] * 6,
        out_specs=VMEM,
        out_shape=jax.ShapeDtypeStruct((width + 8, width), F32),
        name="came_sums",
        **params(16, 32 * width * came.size, 12 * came.size),
    )(met, came, cross, pair, came_turn, own)


def picks_kernel(order_ref, value_ref, carried_ref, picks_ref):
    rows = order_ref.shape[1]
    carried_ref[...] = value_ref[...]
    for start in range(0, rows, LANES):
        here = slice(start, start + LANES)
        place = jnp.broadcast_to(order_ref[:, here], (LANES, LANES)).T
        for lane in range(0, rows, LANES):
            lanes = lane + lax.broadcasted_iota(jnp.int32, (LANES, LANES), 1)
            picks_ref[here, lane:lane + LANES] = jnp.where(place == lanes, 1.0, 0.0).astype(BF16)


def picked(order, value):
    rows = order.shape[1]
    return pl.pallas_call(
        picks_kernel,
        in_specs=[VMEM] * 2,
        out_specs=[VMEM] * 2,
        out_shape=like(value) + [jax.ShapeDtypeStruct((rows, rows), BF16)],
        name="picks",
        **params(8, rows * rows, 2 * rows * rows),
    )(order, value)


def order_kernel(start, stop, picks_ref, split_ref, value_ref, *refs):
    carried_ref, matrix_ref = refs[-2:]
    width = matrix_ref.shape[3]
    carried_ref[...] = value_ref[...]
    both = mul(picks_ref[start:stop, :], split_ref[...], NT)
    for term in range(2):
        for block in range(SLOTS):
            first = (term * SLOTS + block) * width
            matrix_ref[term, block, start:stop, :] = both[:, first:first + width].astype(BF16)


def ordered(picks, split, value, span_of, into=None):
    columns, rows = split.shape[0] // 2, split.shape[1]
    extra = () if into is None else (into,)
    return pl.pallas_call(
        functools.partial(order_kernel, *span_of),
        in_specs=[VMEM] * (3 + len(extra)),
        out_specs=[VMEM] * 2,
        out_shape=like(value) + [jax.ShapeDtypeStruct((2, SLOTS, rows, columns // SLOTS), BF16)],
        input_output_aliases={} if into is None else {3: 1},
        name="row_order",
        **params(16, 4 * columns * rows * (span_of[1] - span_of[0]), 8 * columns * rows),
    )(picks, split, value, *extra)


def behind_kernel(chosen_ref, matrix_ref, rotation_ref, block_ref):
    rows, width = block_ref.shape
    (one, two), turn = places(chosen_ref, rotation_ref)[0]
    turn = halves(turn)
    chunk = rows // PARTS
    for part in range(PARTS):
        here = pl.ds(part * chunk, chunk)
        pair = [
            jnp.concatenate([matrix_ref[term, one, here], matrix_ref[term, two, here]], axis=1) for term in range(2)
        ]
        block_ref[here] = mul_narrow(pair, turn)


def behind_block(chosen, matrix, turns):
    _, _, rows, width = matrix.shape
    return pl.pallas_call(
        behind_kernel,
        in_specs=[SMEM] + [VMEM] * 2,
        out_specs=VMEM,
        out_shape=jax.ShapeDtypeStruct((rows, width), F32),
        name="behind_block",
        **params(16, 12 * rows * width * width, 2 * matrix.size),
    )(chosen, matrix, turns)


def turn_kernel(chosen_ref, matrix_ref, rotation_ref, value_ref, carried_ref, turned_ref):
    rows, width = matrix_ref.shape[2:]
    partner, first, second = pair_slots(chosen_ref[0])
    carried_ref[...] = value_ref[...]
    chunk = rows // PARTS
    for index, (one, two) in enumerate(((partner, SLOTS - 1), (first, second))):
        turn = halves(rotation_ref[index])
        for part in range(PARTS):
            here = pl.ds(part * chunk, chunk)
            pair = [
                jnp.concatenate([matrix_ref[term, one, here], matrix_ref[term, two, here]], axis=1) for term in range(2)
            ]
            for term, half in enumerate(halves(mul_split(pair, turn))):
                turned_ref[term, one, here] = half[:, :width]
                turned_ref[term, two, here] = half[:, width:]

def turn(chosen, matrix, turns, value):
    _, _, rows, width = matrix.shape
    return pl.pallas_call(
        turn_kernel,
        in_specs=[SMEM] + [VMEM] * 3,
        out_specs=[VMEM] * 2,
        out_shape=like(value, matrix),
        name="first_turn",
        **params(16, 24 * rows * width * width, 4 * matrix.size),
    )(chosen, matrix, turns, value)


def moved_kernel(picks_ref, one_ref, two_ref, turn_ref, value_ref, carried_ref, block_ref):
    width = block_ref.shape[2]
    carried_ref[...] = value_ref[...]
    came = jnp.concatenate([one_ref[...], two_ref[...]], axis=1)
    both = mul(picks_ref[...], jnp.concatenate(halves(dot_split(turn_ref[...], came, TN)), axis=0), NT)
    for term in range(2):
        block_ref[term] = both[:, term * width:(term + 1) * width].astype(BF16)


def moved_block(picks, came, came_turn, value):
    rows = picks.shape[0]
    pair, width = came_turn.shape
    return pl.pallas_call(
        moved_kernel,
        in_specs=[VMEM] * 5,
        out_specs=[VMEM] * 2,
        out_shape=like(value) + [jax.ShapeDtypeStruct((2, rows, width), BF16)],
        name="moved_block",
        **params(16, 4 * width * rows * rows, 2 * picks.size),
    )(picks, *came, came_turn, value)


def most_kernel(chosen_ref, turned_ref, moved_ref, rotation_ref, out_ref, ready_ref, sems):
    rows, width = moved_ref.shape[1:]
    meets, low, high = pair_slots(chosen_ref[1])
    chunk = rows // PARTS
    pair_turn = halves(rotation_ref[1])
    meets_turn = halves(rotation_ref[0, :, :width])
    stores = []
    for part in range(PARTS):
        here = pl.ds(part * chunk, chunk)

        def beside(one, two):
            return [jnp.concatenate([one[term], two[term]], axis=1) for term in range(2)]

        def block(slot, here=here):
            return [turned_ref[term, slot, here] for term in range(2)]

        pair = mul_split(beside(block(low), block(high)), pair_turn)
        ready_ref[here, span(low, width)] = pair[:, :width]
        ready_ref[here, span(high, width)] = pair[:, width:]
        ready_ref[here, span(meets, width)] = mul_narrow(
            beside(block(meets), [moved_ref[term, here] for term in range(2)]), meets_turn)
        stores.append(pltpu.make_async_copy(
            ready_ref.at[here], out_ref.at[here, pl.ds(0, (SLOTS - 1) * width)], sems.at[part]))
        stores[-1].start()
    for store in stores:
        store.wait()


def most_slots(chosen, turned, moved, turns):
    _, _, rows, width = turned.shape
    return pl.pallas_call(
        most_kernel,
        in_specs=[SMEM] + [VMEM] * 3,
        out_specs=ANY,
        out_shape=jax.ShapeDtypeStruct((rows, SLOTS * width), F32),
        scratch_shapes=[pltpu.VMEM((rows, (SLOTS - 1) * width), F32), pltpu.SemaphoreType.DMA((PARTS,))],
        name="second_turn",
        **params(16, 18 * rows * width * width, 4 * turned.size),
    )(chosen, turned, moved, turns)


def rest_kernel(turned_ref, behind_ref, turn_ref, _, out_ref, ready_ref, sems):
    rows, width = behind_ref.shape
    chunk = rows // PARTS
    split = halves(turn_ref[...])
    stores = []
    for part in range(PARTS):
        here = pl.ds(part * chunk, chunk)
        pair = [
            jnp.concatenate([one, turned_ref[term, SLOTS - 1, here]], axis=1)
            for term, one in enumerate(halves(behind_ref[here]))
        ]
        ready_ref[here] = mul_narrow(pair, split)
        stores.append(pltpu.make_async_copy(
            ready_ref.at[here], out_ref.at[here, pl.ds((SLOTS - 1) * width, width)], sems.at[part]))
        stores[-1].start()
    for store in stores:
        store.wait()


def last_slot(turned, behind, behind_turn, out):
    _, _, rows, width = turned.shape
    return pl.pallas_call(
        rest_kernel,
        in_specs=[VMEM] * 3 + [ANY],
        out_specs=ANY,
        out_shape=like(out)[0],
        scratch_shapes=[pltpu.VMEM((rows, width), F32), pltpu.SemaphoreType.DMA((PARTS,))],
        input_output_aliases={3: 0},
        name="last_slot",
        **params(16, 12 * rows * width * width, 12 * rows * width),
    )(turned, behind, behind_turn, out)


def from_behind(value, axis, steps):
    count = lax.axis_size(axis)
    pairs = [(source, (source + steps) % count) for source in range(count)]
    return lax.ppermute(value, axis, pairs)


def summed(value, axis, beside):
    count = lax.axis_size(axis)
    got = jnp.zeros_like(value)
    if count & (count - 1):
        value, count = lax.psum(value, axis), 1
    distance = 1
    while distance < count:
        if distance > 1:
            value = value + got
        got = lax.ppermute(value, axis, [(source, source ^ distance) for source in range(count)])
        if beside:
            value = beside.pop(0)(value)
        distance *= 2
    for work in beside:
        value = work(value)
    return value, got


def both_summed(one, two, axis, beside):
    count = lax.axis_size(axis)
    one, two = lax.optimization_barrier((one, two))
    values, got = [one, two], [jnp.zeros_like(one), jnp.zeros_like(two)]
    if count & (count - 1):
        values, count = [lax.psum(value, axis) for value in values], 1
    d = [1 << bit for bit in range(count.bit_length() - 1)]
    for place, distances in enumerate(zip(*(d[:1] + d[:0:-1], d[::-1]))):
        if place:
            values = [value + came for value, came in zip(values, got)]
        got = [
            lax.ppermute(value, axis, [(source, source ^ distance) for source in range(count)])
            for value, distance in zip(values, distances)
        ]
        if beside:
            values[0] = beside.pop(0)(values[0])
    for work in beside:
        values[0] = work(values[0])
    return values[0], got[0], values[1], got[1]


def body(tracks, pixel_order, pairing):
    frames_dev, _, pixel_total = tracks.shape
    row_devices = lax.axis_size("rows")
    row_count = pixel_total // row_devices
    pieces = spread(tracks, row_devices).reshape(row_devices * 4, frames_dev // 2, row_count)
    arrived = lax.all_to_all(pieces, ("rows", "cols"), split_axis=0, concat_axis=0, tiled=True)
    held = arrived.reshape(-1, row_count)
    order = (pixel_order - lax.axis_index("rows") * row_count).reshape(1, row_count)
    chosen = lax.dynamic_index_in_dim(pairing, lax.axis_index("cols"), axis=1, keepdims=False)
    part = row_count * 3 // 8
    kept = {}

    def gram_work(value):
        value, kept["gram"], kept["split"] = local_gram(value, tiles)
        return value

    def order_first(value):
        value, kept["picks"] = picked(order, value)
        value, kept["matrix"] = ordered(kept["picks"], kept["split"], value, (0, part))
        return value

    def order_rest(value):
        value, kept["matrix"] = ordered(kept["picks"], kept["split"], value, (part, row_count), kept["matrix"])
        return value

    def turn_work(value):
        value, kept["turned"] = turn(chosen, kept["matrix"], turns, value)
        return value

    def moved_work(value):
        value, kept["moved"] = moved_block(kept["picks"], came, came_turn, value)
        return value

    sums, *last, tiles = couplings(chosen, held)
    came = [from_behind(half, "cols", 1) for half in last]
    turns, sent = two_rotations(*summed(sums, "rows", [gram_work, order_first, order_rest]))
    came_turn = from_behind(sent, "cols", 1)
    behind_sent = behind_block(chosen, kept["matrix"], turns)
    own, met, cross, pair = meet(chosen, kept["gram"], kept["split"], came[0], turns, behind_sent)
    behind = from_behind(lax.optimization_barrier((behind_sent, came_turn, met))[0], "cols", -1)
    sums = came_sums(met, came[1], cross, pair, came_turn, own)

    second_turns, sent = two_rotations(*both_summed(sums, own, "rows", [moved_work, turn_work]))
    behind_turn = from_behind(sent, "cols", -1)
    out = most_slots(chosen, kept["turned"], kept["moved"], second_turns)
    return last_slot(kept["turned"], behind, behind_turn, out)


def solution(mesh):
    placed = (P(("rows", "cols"), None, None), P("rows"), P())
    return jax.shard_map(
        body, mesh=mesh, in_specs=placed, out_specs=P("rows", "cols"), check_vma=False
    )
```
